32 devices in a mesh: dp: 8 (over z, x), rep: 4 (over y, core).
Axes of the slice: x: 2, y: 2, z: 4, core: 2. Of those that a mesh axis runs over, the one named last changes fastest.
Arguments:
- feats: bfloat16 [3072, 4, 4, 512], P(('dp', 'rep')), may hold values from -6 to 6
- labels: int32 [3072], P(('dp', 'rep')), may hold values from 0 to 9
- task_ids: int32 [3072], P(('dp', 'rep')), may hold values from 0 to 9, as said below
- live: int32 [3072], P(('dp', 'rep')), may hold values from 0 to 1, as said below
- branch: int32 [3072], P(('dp', 'rep')), may hold values from 0 to 1, as said below
- mem_counts: int32 [9], replicated, may hold values from 20 to 256
- conv_master: float32 [2, 4608, 512], P(None, None, 'rep'), may hold values from -0.09375 to 0.09375
- conv_rows: float32 [2, 4608], replicated, may hold values from 9.765625e-09 to 3.90625e-08
- conv_cols: float32 [2, 512], P(None, 'rep'), may hold values from 9.765625e-09 to 3.90625e-08
- head_master: float32 [512, 100], replicated, may hold values from -0.26516504 to 0.26516504
- head_rows: float32 [512], replicated, may hold values from 8.138021e-07 to 3.2552084e-06
- head_cols: float32 [100], replicated, may hold values from 8.138021e-06 to 3.2552085e-05
- head_bias: float32 [100], replicated, may hold values from -1.8 to 1.8
- head_bias_moment: float32 [100], replicated, may hold values from 2.2786458e-05 to 9.1145834e-05
- norm_gain: float32 [2, 512], replicated, may hold values from 0.25 to 2
- norm_bias: float32 [2, 512], replicated, may hold values from -1.8 to 1.8
- norm_moment: float32 [2, 2, 512], replicated, may hold values from 2.6041667e-08 to 1.04166666e-07
Outputs:
- cur_losses: float32 [2], replicated
- mem_losses: float32 [2], replicated
- agreement: float32 [2], replicated
- conv_grad: float32 [2, 4608, 512], P(None, None, 'rep')
- conv_rows_new: float32 [2, 4608], replicated
- conv_cols_new: float32 [2, 512], P(None, 'rep')
- conv_new: float32 [2, 4608, 512], P(None, None, 'rep')
- conv_copy_new: bfloat16 [2, 4608, 512], P(None, None, 'rep')
- head_grad: float32 [512, 100], replicated
- head_rows_new: float32 [512], replicated
- head_cols_new: float32 [100], replicated
- head_new: float32 [512, 100], replicated
- head_copy_new: bfloat16 [512, 100], replicated
- head_bias_grad: float32 [100], replicated
- head_bias_moment_new: float32 [100], replicated
- head_bias_new: float32 [100], replicated
- norm_grad: float32 [2, 2, 512], replicated
- norm_moment_new: float32 [2, 2, 512], replicated
- norm_new: float32 [2, 2, 512], replicated
The draws below stay inside these ranges and needn't reach their ends.
Inputs may be any that keep to these rules, and one draw needn't show every extreme that they name: Each device's first two rows are live. `branch`: each device's first row is a current row and its second a memory row. `task_ids`: memory rows name past tasks 0 to 8; current rows name task 10 - 1.
All inputs are finite; a program needn't handle non-finite values.
Results may differ from the reference program's by a relative error of at most 0.015.
Values may be sent and summed in bfloat16 or wider, within the bound.
No kernel may reach another device: no remote copies, remote signals or barrier semaphores. Data moves between devices by JAX's collectives and lax.ppermute only.
A program may use at most 256 MiB of HBM per device.

```python
import math
import jax
import jax.numpy as jnp
from jax import lax

C = 512
PIX = 4
CLASSES = 10
TASKS = 10
STEP = 10
SAMP_DEV = 96
N_DP = 8
N_REP = 4


def row_plan(key):
    total_rows = SAMP_DEV * N_DP * N_REP
    pair_count = total_rows // 2
    parity = jnp.arange(total_rows) % 2
    pair_slot = 2 * jnp.arange(pair_count) % SAMP_DEV
    flips = jax.random.randint(jax.random.fold_in(key, 11), (pair_count,), 0, 2)
    flips = jnp.where(pair_slot == 0, 0, flips)
    spread = jnp.repeat(flips, 2)
    kinds = jnp.where(spread == 1, 1 - parity, parity)
    earlier = jax.random.randint(jax.random.fold_in(key, 12), (total_rows,), 0, TASKS - 1)
    task_list = jnp.where(kinds == 1, earlier, TASKS - 1)
    return (kinds.astype(jnp.int32), task_list.astype(jnp.int32), flips.astype(jnp.int32))


def draw_branch(key, part):
    kinds, task_list, flips = row_plan(key)
    return kinds


def draw_task_ids(key, part):
    kinds, task_list, flips = row_plan(key)
    return task_list


def draw_live(key, part):
    key = jax.random.fold_in(key, 5)
    total_rows = SAMP_DEV * N_DP * N_REP
    row_index = jnp.arange(total_rows)
    device = row_index // SAMP_DEV
    slot_index = row_index % SAMP_DEV
    along = device // N_REP * (N_REP - 1) + device % N_REP * (N_DP - 1)
    span_total = 2 * (N_DP - 1) * (N_REP - 1)
    permille = 100 + 800 * along // span_total
    rolled = jnp.repeat(jax.random.randint(key, (total_rows // 2,), 0, 1000), 2)
    return jnp.where((rolled < permille) | (slot_index < 2), 1, 0).astype(jnp.int32)


def draw_labels(key, part):
    key = jax.random.fold_in(key, 9)
    total_rows = SAMP_DEV * N_DP * N_REP
    paired = jax.random.randint(key, (total_rows // 2,), 0, CLASSES)
    return jnp.repeat(paired, 2).astype(jnp.int32)


def draw_feats(key, part):
    kinds, task_list, flips = row_plan(key)
    key = jax.random.fold_in(key, 7)
    total_rows = SAMP_DEV * N_DP * N_REP
    shape = (total_rows // 2, 2, PIX, PIX, C)
    base = jnp.clip(jax.random.normal(key, shape, jnp.float32), -4.0, 4.0)
    current = base[:, 0]
    memory = 0.8 * base[:, 0] + 0.6 * base[:, 1]
    flag = flips[:, None, None, None] == 1
    first = jnp.where(flag, memory, current)
    second = jnp.where(flag, current, memory)
    return jnp.stack([first, second], axis=1).reshape(total_rows, PIX, PIX, C).astype(jnp.bfloat16)


def draw_head_master(key, part):
    key = jax.random.fold_in(key, 8)
    shape = (C, TASKS, CLASSES)
    base = jnp.clip(jax.random.normal(key, shape, jnp.float32), -4.0, 4.0)
    base = base * C ** (-0.5)
    last = base[:, TASKS - 1:]
    others = -0.8 * last + 0.6 * base[:, :TASKS - 1]
    return jnp.concatenate([others, last], axis=1).reshape(C, TASKS * CLASSES)


def draw_norm_gain(key, part):
    key = jax.random.fold_in(key, 6)
    placed = jnp.arange(C).astype(jnp.float32) / (C - 1)
    rising = 0.5 + placed
    jitter = jax.random.uniform(key, (2, C), jnp.float32, 0.9, 1.1)
    return rising[None, :] * jitter


def with_ends(array, rng, least, largest):
    place = [jax.random.randint(jax.random.fold_in(rng, axis), (), 0, length) for axis, length in enumerate(array.shape)]
    longest = array.shape.index(max(array.shape))
    neighbour = place[:longest] + [(place[longest] + 1) % array.shape[longest]] + place[longest + 1:]
    return array.at[tuple(place)].set(least).at[tuple(neighbour)].set(largest)


def levels(key, extent, cuts, low, top_value):
    def one(axis_at, parts):
        draws = jax.random.uniform(jax.random.fold_in(jax.random.fold_in(key, 6), axis_at), (parts,), jnp.float32, low / len(cuts), top_value / len(cuts))
        return jnp.repeat(jnp.exp(draws), extent[axis_at] // parts).reshape((-1,) + (1,) * (len(extent) - axis_at - 1))

    factor_of = one(*cuts[0])
    for cut in cuts[1:]:
        factor_of = factor_of * one(*cut)
    return factor_of


def scatter_about(key, extent, scale, most, cuts=(), kind=jnp.bfloat16):
    entries = scale * jax.random.normal(key, extent, jnp.float32)
    if cuts:
        entries = entries * levels(key, extent, cuts, -0.22, 0.18)
    return jnp.clip(entries, -most, most).astype(kind)


def setup_inputs(seed: int = 0) -> dict:
    keys = jax.random.split(jax.random.key(seed), 18)
    return {
        "feats": draw_feats(jax.random.fold_in(keys[17], 71), 0),
        "labels": draw_labels(jax.random.fold_in(keys[17], 71), 0),
        "task_ids": draw_task_ids(jax.random.fold_in(keys[17], 71), 0),
        "live": draw_live(jax.random.fold_in(keys[17], 71), 0),
        "branch": draw_branch(jax.random.fold_in(keys[17], 71), 0),
        "mem_counts": with_ends(jax.random.randint(keys[5], (TASKS - 1,), 20, 257), jax.random.fold_in(keys[5], 1), 20, 256).astype(jnp.int32),
        "conv_master": scatter_about(keys[6], (2, 9 * C, C), (9 * C) ** -0.5, 0.09375, ((2, 4),), jnp.float32),
        "conv_rows": jnp.clip(jnp.exp(jax.random.uniform(keys[7], (2, 9 * C), jnp.float32, math.log(9.765624753299562e-09), math.log(3.906249901319825e-08))), 9.765624753299562e-09, 3.906249901319825e-08),
        "conv_cols": jnp.clip(jnp.exp(math.log(3.906249901319825e-08) - 1.3862944 * jax.random.uniform(keys[8], (2, C), jnp.float32) ** levels(keys[8], (2, C), ((1, 4),), -0.2, 0.2)), 9.765624753299562e-09, 3.906249901319825e-08),
        "head_master": draw_head_master(jax.random.fold_in(keys[17], 71), 0),
        "head_rows": jnp.clip(jnp.exp(jax.random.uniform(keys[10], (C,), jnp.float32, math.log(8.138021030390519e-07), math.log(3.2552084121562075e-06))), 8.138021030390519e-07, 3.2552084121562075e-06),
        "head_cols": jnp.clip(jnp.exp(jax.random.uniform(keys[11], (TASKS * CLASSES,), jnp.float32, math.log(8.138021257764194e-06), math.log(3.255208503105678e-05))), 8.138021257764194e-06, 3.255208503105678e-05),
        "head_bias": scatter_about(keys[12], (TASKS * CLASSES,), 0.3, 1.8, (), jnp.float32),
        "head_bias_moment": jnp.clip(jnp.exp(jax.random.uniform(keys[13], (TASKS * CLASSES,), jnp.float32, math.log(2.27864584303461e-05), math.log(9.11458337213844e-05))), 2.27864584303461e-05, 9.11458337213844e-05),
        "norm_gain": draw_norm_gain(jax.random.fold_in(keys[17], 71), 0),
        "norm_bias": scatter_about(keys[15], (2, C), 0.3, 1.8, (), jnp.float32),
        "norm_moment": jnp.clip(jnp.exp(jax.random.uniform(keys[16], (2, 2, C), jnp.float32, math.log(2.604166660091778e-08), math.log(1.0416666640367112e-07))), 2.604166660091778e-08, 1.0416666640367112e-07),
    }


@jax.custom_vjp
def low(v):
    return lax.optimization_barrier(v.astype(jnp.bfloat16)).astype(jnp.float32)

@jax.custom_vjp
def low_back(v):
    return v

def low_keep(v):
    return (low(v), None)

def low_pass(kept, grad):
    return (grad,)

def back_keep(v):
    return (v, None)

def back_low(kept, grad):
    return (low(grad),)
low.defvjp(low_keep, low_pass)
low_back.defvjp(back_keep, back_low)
norm_eps = 1e-05
eps_one = 1e-30
eps_two = 0.001
rel_step = 0.5
clip_level = 1.0

def shifted(feature_map, row_off, col_off):
    padded = jnp.pad(feature_map, ((0, 0), (1, 1), (1, 1), (0, 0)))
    return padded[:, row_off:row_off + PIX, col_off:col_off + PIX, :]

def convolve(feature_map, kernel):
    running = jnp.zeros(feature_map.shape, jnp.float32)
    for tap_index in range(9):
        window = shifted(feature_map, tap_index // 3, tap_index % 3)
        running = running + jnp.einsum('spqc,cd->spqd', window, kernel[tap_index * C:(tap_index + 1) * C], precision=lax.Precision.HIGHEST)
    return running

def normalize(hidden, live_rows, norm_count, gain, bias):
    masked = hidden * live_rows
    mean_val = lax.optimization_barrier(jnp.sum(masked, axis=(0, 1, 2))) / norm_count
    square = lax.optimization_barrier(jnp.sum(masked * hidden, axis=(0, 1, 2))) / norm_count
    return (hidden - mean_val) * lax.rsqrt(square - mean_val * mean_val + norm_eps) * gain + bias

def forward(conv_w, head_w, head_b, gains, biases, feature_map, live_rows, norm_count, task_hot, label_hot, weights):
    kernel = low(conv_w)
    first_map = low_back(convolve(feature_map, kernel[0]))
    activated = low(jax.nn.silu(normalize(first_map, live_rows, norm_count, gains[0], biases[0])))
    second_map = low_back(convolve(activated, kernel[1]))
    block_out = jax.nn.silu(feature_map + normalize(second_map, live_rows, norm_count, gains[1], biases[1]))
    pooled = low(lax.optimization_barrier(jnp.mean(block_out, axis=(1, 2))))
    logits = low_back(jnp.dot(pooled, low(head_w), precision=lax.Precision.HIGHEST) + head_b)
    chosen = lax.optimization_barrier(jnp.sum(logits.reshape(-1, TASKS, CLASSES) * task_hot[:, :, None], axis=1))
    row_top = lax.optimization_barrier(jnp.max(chosen, axis=1, keepdims=True))
    entropy = row_top[:, 0] + jnp.log(lax.optimization_barrier(jnp.sum(jnp.exp(chosen - row_top), axis=1))) - lax.optimization_barrier(jnp.sum(chosen * label_hot, axis=1))
    return jnp.dot(weights, entropy, precision=lax.Precision.HIGHEST)

def factored(weight, grad_mat, row_stat, col_stat, decay_rate):
    square = grad_mat * grad_mat + eps_one
    new_rows = decay_rate * row_stat + (1.0 - decay_rate) * lax.optimization_barrier(jnp.mean(square, axis=-1))
    new_cols = decay_rate * col_stat + (1.0 - decay_rate) * lax.optimization_barrier(jnp.mean(square, axis=-2))
    second_est = new_rows[..., :, None] * new_cols[..., None, :] / lax.optimization_barrier(jnp.mean(new_rows, axis=-1))[..., None, None]
    update = grad_mat * lax.rsqrt(second_est)
    update = update / jnp.maximum(1.0, jnp.sqrt(lax.optimization_barrier(jnp.mean(update * update, axis=(-2, -1), keepdims=True))) / clip_level)
    step_size = rel_step * jnp.maximum(eps_two, jnp.sqrt(lax.optimization_barrier(jnp.mean(weight * weight, axis=(-2, -1), keepdims=True))))
    return (new_rows, new_cols, weight - step_size * update)

def plain(weight, grad_vec, moment, decay_rate):
    new_moment = decay_rate * moment + (1.0 - decay_rate) * (grad_vec * grad_vec + eps_one)
    update = grad_vec * lax.rsqrt(new_moment)
    update = update / jnp.maximum(1.0, jnp.sqrt(lax.optimization_barrier(jnp.mean(update * update, axis=-1, keepdims=True))) / clip_level)
    step_size = rel_step * jnp.maximum(eps_two, jnp.sqrt(lax.optimization_barrier(jnp.mean(weight * weight, axis=-1, keepdims=True))))
    return (new_moment, weight - step_size * update)

def reference(feats, labels, task_ids, live, branch, mem_counts, conv_master, conv_rows, conv_cols, head_master, head_rows, head_cols, head_bias, head_bias_moment, norm_gain, norm_bias, norm_moment):
    feature_map = feats.astype(jnp.float32)
    live_rows = live.astype(jnp.float32)
    memory = branch.astype(jnp.float32)
    past_tasks = jnp.arange(TASKS - 1)
    inverse = lax.optimization_barrier(jnp.sum(jnp.where(task_ids[:, None] == past_tasks[None, :], 1.0 / mem_counts.astype(jnp.float32)[None, :], 0.0), axis=1))
    cur_weight = live_rows * (1.0 - memory)
    mem_weight = live_rows * memory * inverse
    weights = jnp.stack([cur_weight, mem_weight])
    totals = lax.optimization_barrier(jnp.sum(weights, axis=1))
    norm_count = PIX * PIX * jnp.sum(live_rows)
    task_hot = (task_ids[:, None] == jnp.arange(TASKS)[None, :]).astype(jnp.float32)
    label_hot = (labels[:, None] == jnp.arange(CLASSES)[None, :]).astype(jnp.float32)

    def objective(conv_w, head_w, head_b, gains, biases):
        return forward(conv_w, head_w, head_b, gains, biases, feature_map, live_rows[:, None, None, None], norm_count, task_hot, label_hot, weights)
    loss_sums, pullback = jax.vjp(objective, conv_master, head_master, head_bias, norm_gain, norm_bias)
    nothing = jnp.zeros((), jnp.float32)
    grad_cur = pullback(jnp.stack([1.0 / totals[0], nothing]))
    grad_ref = pullback(jnp.stack([nothing, 1.0 / totals[1]]))
    inner_dot = sum((jnp.sum(first_part * other_part) for first_part, other_part in zip(grad_cur, grad_ref)))
    ref_square = sum((jnp.sum(other_part * other_part) for other_part in grad_ref))
    project_coef = jnp.minimum(inner_dot, 0.0) / ref_square
    conv_grad, head_grad, bias_grad, gain_grad, shift_grad = [first_part - project_coef * other_part for first_part, other_part in zip(grad_cur, grad_ref)]
    decay_rate = 1.0 - STEP ** (-0.8)
    conv_rows_new, conv_cols_new, conv_new = factored(conv_master, conv_grad, conv_rows, conv_cols, decay_rate)
    head_rows_new, head_cols_new, head_new = factored(head_master, head_grad, head_rows, head_cols, decay_rate)
    bias_moment_new, bias_new = plain(head_bias, bias_grad, head_bias_moment, decay_rate)
    norm_grad = jnp.stack([gain_grad, shift_grad])
    norm_moment_new, norm_new = plain(jnp.stack([norm_gain, norm_bias]), norm_grad, norm_moment, decay_rate)
    cur_losses = jnp.stack([loss_sums[0], totals[0]])
    mem_losses = jnp.stack([loss_sums[1], totals[1]])
    agreement = jnp.stack([inner_dot, ref_square])
    return (cur_losses, mem_losses, agreement, conv_grad, conv_rows_new, conv_cols_new, conv_new, conv_new.astype(jnp.bfloat16), head_grad, head_rows_new, head_cols_new, head_new, head_new.astype(jnp.bfloat16), bias_grad, bias_moment_new, bias_new, norm_grad, norm_moment_new, norm_new)
```

```python
import jax
import jax.numpy as jnp
from jax import lax
from jax.sharding import PartitionSpec as P

CLASSES = 10
TASKS = 10
STEP = 10


norm_eps = 1e-05
eps_one = 1e-30
eps_two = 0.001
rel_step = 0.5
clip_level = 1.0


def swap(x, axis, bit):
    n = lax.axis_size(axis)
    return lax.ppermute(x, axis, [(i, i ^ bit) for i in range(n)])


def bits_of(n):
    return [1 << k for k in range(n.bit_length() - 1)]


def exchange_sum(x, axis, basis):
    first = x + swap(x, axis, basis[0]) if len(basis) == 1 else None
    if first is not None:
        return first
    a, b = basis
    return (x + swap(x, axis, a)) + (swap(x, axis, b) + swap(x, axis, a ^ b))


def axis_sum(x, axis):
    bits = bits_of(lax.axis_size(axis))
    if len(bits) % 2:
        x = exchange_sum(x, axis, bits[:1])
        bits = bits[1:]
    while bits:
        x = exchange_sum(x, axis, bits[:2])
        bits = bits[2:]
    return x


def all_sum(x):
    return axis_sum(axis_sum(x, "rep"), "dp")


def coord(axis, bit):
    return (lax.axis_index(axis) & bit) // bit


def pick(x, dim, index):
    return lax.dynamic_index_in_dim(x, index, dim, keepdims=False)


def halve(x, dim, axis, bit):
    mine = coord(axis, bit)
    other = swap(pick(x, dim, 1 - mine), axis, bit)
    return (pick(x, dim, mine).astype(jnp.float32) + other.astype(jnp.float32)).astype(x.dtype)


def double(x, dim, axis, bit):
    other = swap(x, axis, bit)
    mine = coord(axis, bit) == 0
    return jnp.stack([jnp.where(mine, x, other), jnp.where(mine, other, x)], axis=dim)


def orders(nrep, ndp):
    rep_bits = [("rep", b) for b in bits_of(nrep)]
    dp_bits = [("dp", b) for b in bits_of(ndp)]
    core, rest = rep_bits[:1], rep_bits[1:]
    return [
        core + rest + dp_bits,
        core + dp_bits[:1] + rest + dp_bits[1:],
        core + dp_bits[1:] + dp_bits[:1] + rest,
    ]


def labels_of(nrep, ndp):
    return [("rep", b) for b in reversed(bits_of(nrep))] + [("dp", b) for b in reversed(bits_of(ndp))]


def scatter(x, order, nrep, ndp):
    names = labels_of(nrep, ndp)
    for key in order:
        dim = names.index(key)
        x = halve(x, dim, *key)
        names.pop(dim)
    return x


def gather_dp(x, order, ndp):
    target = [("dp", b) for b in reversed(bits_of(ndp))]
    names = []
    for key in reversed([k for k in order if k[0] == "dp"]):
        dim = sum(target.index(n) < target.index(key) for n in names)
        x = double(x, dim, *key)
        names.insert(dim, key)
    return x


def convolve(feature_map, kernel):
    channels = feature_map.shape[3]
    map_side = feature_map.shape[0]
    padded = jnp.pad(feature_map, ((1, 1), (1, 1), (0, 0), (0, 0)))
    running = 0.0
    for tap_index in range(9):
        row_off = tap_index // 3
        col_off = tap_index % 3
        window = padded[row_off : row_off + map_side, col_off : col_off + map_side]
        running = running + jnp.einsum(
            "pqsc,cd->pqsd",
            window,
            kernel[tap_index * channels : (tap_index + 1) * channels],
            preferred_element_type=jnp.float32,
        )
    return running


def convolve_back(grad_map, kernel):
    channels = grad_map.shape[4]
    map_side = grad_map.shape[1]
    padded = jnp.pad(grad_map, ((0, 0), (1, 1), (1, 1), (0, 0), (0, 0)))
    running = 0.0
    for tap_index in range(9):
        row_off = 2 - tap_index // 3
        col_off = 2 - tap_index % 3
        window = padded[:, row_off : row_off + map_side, col_off : col_off + map_side]
        running = running + jnp.einsum(
            "tpqsd,cd->tpqsc",
            window,
            kernel[tap_index * channels : (tap_index + 1) * channels],
            preferred_element_type=jnp.float32,
        )
    return running


def layer_grad(feature_map, grad_map, nrep, ndp):
    map_side = feature_map.shape[0]
    channels = feature_map.shape[3]
    padded = jnp.pad(feature_map, ((1, 1), (1, 1), (0, 0), (0, 0)))
    shards = []
    for part, order in enumerate(orders(nrep, ndp)):
        pieces = []
        for tap_index in range(3 * part, 3 * part + 3):
            row_off = tap_index // 3
            col_off = tap_index % 3
            window = padded[row_off : row_off + map_side, col_off : col_off + map_side]
            pieces.append(
                jnp.einsum("pqsc,tpqsd->tcd", window, grad_map, preferred_element_type=jnp.float32)
            )
        block = jnp.stack(pieces).astype(jnp.bfloat16)
        block = block.reshape(3, 2, ndp, channels // ndp, nrep, channels // nrep)
        block = block.transpose(4, 2, 0, 1, 3, 5)
        lead = [2] * (len(bits_of(nrep)) + len(bits_of(ndp)))
        shards.append(scatter(block.reshape(*lead, *block.shape[2:]), order, nrep, ndp))
    return shards


def silu_slope(inputs):
    sig_gate = jax.nn.sigmoid(inputs)
    return sig_gate * (1.0 + inputs * (1.0 - sig_gate))


def moments(hidden, live_rows):
    masked = hidden * live_rows[None, None, :, None]
    return jnp.stack([jnp.sum(masked, axis=(0, 1, 2)), jnp.sum(masked * hidden, axis=(0, 1, 2))])


def norm_apply(hidden, stat_sum, stat_square, norm_count, gain, bias):
    mean_val = stat_sum / norm_count
    norm_scale = lax.rsqrt(stat_square / norm_count - mean_val * mean_val + norm_eps)
    normed = (hidden - mean_val) * norm_scale
    return (normed, norm_scale, normed * gain + bias)


def norm_back(upstream, normed, norm_scale, gain, live_rows, norm_count):
    local_bias = jnp.sum(upstream, axis=(1, 2, 3))
    local_gain = jnp.sum(upstream * normed, axis=(1, 2, 3))
    bias_grad, gain_grad = all_sum(jnp.stack([local_bias, local_gain]))
    centered = (
        upstream
        - (bias_grad[:, None, None, None, :] + normed * gain_grad[:, None, None, None, :])
        / norm_count
    )
    hidden_grad = centered * (gain * norm_scale) * live_rows[None, None, None, :, None]
    return (hidden_grad.astype(jnp.bfloat16), gain_grad, bias_grad)


def factored(weight, grad_mat, row_stat, col_stat, decay_rate):
    square = grad_mat * grad_mat + eps_one
    new_rows = decay_rate * row_stat + (1.0 - decay_rate) * jnp.mean(square, axis=-1)
    new_cols = decay_rate * col_stat + (1.0 - decay_rate) * jnp.mean(square, axis=-2)
    second_est = (
        new_rows[..., :, None]
        * new_cols[..., None, :]
        / jnp.mean(new_rows, axis=-1)[..., None, None]
    )
    update = grad_mat * lax.rsqrt(second_est)
    update = update / jnp.maximum(
        1.0, jnp.sqrt(jnp.mean(update * update, axis=(-2, -1), keepdims=True)) / clip_level
    )
    step_size = rel_step * jnp.maximum(
        eps_two, jnp.sqrt(jnp.mean(weight * weight, axis=(-2, -1), keepdims=True))
    )
    return (new_rows, new_cols, weight - step_size * update)


def plain(weight, grad_vec, moment, decay_rate):
    new_moment = decay_rate * moment + (1.0 - decay_rate) * (grad_vec * grad_vec + eps_one)
    update = grad_vec * lax.rsqrt(new_moment)
    update = update / jnp.maximum(
        1.0, jnp.sqrt(jnp.mean(update * update, axis=-1, keepdims=True)) / clip_level
    )
    step_size = rel_step * jnp.maximum(
        eps_two, jnp.sqrt(jnp.mean(weight * weight, axis=-1, keepdims=True))
    )
    return (new_moment, weight - step_size * update)


def gather_kernels(lowered, nrep):
    held = lowered[None]
    for bit in reversed(bits_of(nrep)):
        other = swap(held, "rep", bit)
        low = coord("rep", bit) == 0
        held = jnp.stack([jnp.where(low, held, other), jnp.where(low, other, held)], axis=1)
        held = held.reshape((-1,) + lowered.shape)
    return held.transpose(1, 0, 2).reshape(lowered.shape[0], -1)


def local(
    nrep,
    ndp,
    feats,
    labels,
    task_ids,
    live,
    branch,
    mem_counts,
    conv_master,
    conv_rows,
    conv_cols,
    head_master,
    head_rows,
    head_cols,
    head_bias,
    head_bias_moment,
    norm_gain,
    norm_bias,
    norm_moment,
):
    channels = feats.shape[3]
    map_side = feats.shape[1]
    area = map_side * map_side
    decay_rate = 1.0 - STEP ** (-0.8)
    live_rows = live.astype(jnp.float32)
    memory = branch.astype(jnp.float32)
    past_tasks = jnp.arange(TASKS - 1)
    inverse = jnp.sum(
        jnp.where(
            task_ids[:, None] == past_tasks[None, :],
            1.0 / mem_counts.astype(jnp.float32)[None, :],
            0.0,
        ),
        axis=1,
    )
    cur_weight = live_rows * (1.0 - memory)
    mem_weight = live_rows * memory * inverse
    weights = jnp.stack([cur_weight, mem_weight])
    local_counts = jnp.stack([jnp.sum(live_rows), jnp.sum(cur_weight), jnp.sum(mem_weight)])
    kernel_one = gather_kernels(conv_master[0].astype(jnp.bfloat16), nrep)
    kernel_two = gather_kernels(conv_master[1].astype(jnp.bfloat16), nrep)
    head_lowered = head_master.astype(jnp.bfloat16)
    feats_pos = feats.transpose(1, 2, 0, 3)
    first_map = convolve(feats_pos, kernel_one)
    stats = moments(first_map, live_rows)
    packed = jnp.concatenate([stats.reshape(-1), local_counts])
    packed = all_sum(jnp.pad(packed, (0, -packed.shape[0] % 128)))
    stat_sum = packed[:channels]
    stat_square = packed[channels : 2 * channels]
    totals = packed[2 * channels : 2 * channels + 3]
    norm_count = area * totals[0]
    normed_one, scale_one, pre_one = norm_apply(
        first_map, stat_sum, stat_square, norm_count, norm_gain[0], norm_bias[0]
    )
    activated = jax.nn.silu(pre_one).astype(jnp.bfloat16)
    second_map = convolve(activated, kernel_two)
    two_sum, two_square = all_sum(moments(second_map, live_rows))
    normed_two, scale_two, pre_two = norm_apply(
        second_map, two_sum, two_square, norm_count, norm_gain[1], norm_bias[1]
    )
    joined = feats_pos.astype(jnp.float32) + pre_two
    block_out = jax.nn.silu(joined)
    pooled = (jnp.sum(block_out, axis=(0, 1)) / area).astype(jnp.bfloat16)
    logits = jnp.dot(pooled, head_lowered, preferred_element_type=jnp.float32) + head_bias
    task_hot = (task_ids[:, None] == jnp.arange(TASKS)[None, :]).astype(jnp.float32)
    label_hot = (labels[:, None] == jnp.arange(CLASSES)[None, :]).astype(jnp.float32)
    chosen = jnp.sum(logits.reshape(-1, TASKS, CLASSES) * task_hot[:, :, None], axis=1)
    row_top = jnp.max(chosen, axis=1, keepdims=True)
    exp_terms = jnp.exp(chosen - row_top)
    exp_total = jnp.sum(exp_terms, axis=1, keepdims=True)
    entropy = row_top[:, 0] + jnp.log(exp_total[:, 0]) - jnp.sum(chosen * label_hot, axis=1)
    loss_terms = jnp.sum(weights * entropy[None, :], axis=1)
    scales = weights * (1.0 / jnp.stack([totals[1], totals[2]]))[:, None]
    dchosen = (exp_terms / exp_total - label_hot)[None] * scales[:, :, None]
    dlogits = (
        (dchosen[:, :, None, :] * task_hot[None, :, :, None])
        .reshape(2, -1, TASKS * CLASSES)
        .astype(jnp.bfloat16)
    )
    dpooled = jnp.einsum("tsk,ck->tsc", dlogits, head_lowered, preferred_element_type=jnp.float32)
    head_part = jnp.einsum("sc,tsk->tck", pooled, dlogits, preferred_element_type=jnp.float32)
    bias_part = jnp.sum(dlogits.astype(jnp.float32), axis=1)
    upstream = (dpooled / area)[:, None, None, :, :] * silu_slope(joined)[None]
    hidden_two, gain_two, shift_two = norm_back(
        upstream, normed_two, scale_two, norm_gain[1], live_rows, norm_count
    )
    shards_two = layer_grad(activated, hidden_two, nrep, ndp)
    act_grad = convolve_back(hidden_two, kernel_two) * silu_slope(pre_one)[None]
    hidden_one, gain_one, shift_one = norm_back(
        act_grad, normed_one, scale_one, norm_gain[0], live_rows, norm_count
    )
    shards_one = layer_grad(feats_pos, hidden_one, nrep, ndp)
    head_pack = jnp.concatenate(
        [head_part.transpose(1, 0, 2).reshape(channels, -1)]
        + [jnp.zeros((channels, -2 * TASKS * CLASSES % 128), jnp.float32)],
        axis=1,
    )
    tail = jnp.concatenate([bias_part.reshape(-1), loss_terms])
    tail = jnp.pad(tail, (0, head_pack.shape[1] * 8 - tail.shape[0])).reshape(8, -1)
    head_pack = all_sum(jnp.concatenate([head_pack, tail], axis=0))
    tail = head_pack[channels:].reshape(-1)
    head_sum = head_pack[:channels, : 2 * TASKS * CLASSES].reshape(channels, 2, -1).transpose(1, 0, 2)
    bias_sum = tail[: 2 * TASKS * CLASSES].reshape(2, -1)
    loss_sum = tail[2 * TASKS * CLASSES : 2 * TASKS * CLASSES + 2]
    norm_both = jnp.stack(
        [jnp.stack([gain_one, gain_two], axis=1), jnp.stack([shift_one, shift_two], axis=1)], axis=1
    )
    small_dot = (
        jnp.sum(head_sum[0] * head_sum[1])
        + jnp.sum(bias_sum[0] * bias_sum[1])
        + jnp.sum(norm_both[0] * norm_both[1])
    )
    small_square = (
        jnp.sum(head_sum[1] * head_sum[1])
        + jnp.sum(bias_sum[1] * bias_sum[1])
        + jnp.sum(norm_both[1] * norm_both[1])
    )
    parts = [[s.astype(jnp.float32) for s in shards] for shards in (shards_one, shards_two)]
    flat = [s for shards in parts for s in shards]
    partial_value = jnp.stack(
        [
            sum(jnp.sum(s[:, 0] * s[:, 1]) for s in flat),
            sum(jnp.sum(s[:, 1] * s[:, 1]) for s in flat),
        ]
    )
    partial_value = jnp.broadcast_to(partial_value[:, None], (2, 128))
    agreement = all_sum(partial_value)[:, 0] + jnp.stack([small_dot, small_square])
    project_coef = jnp.minimum(agreement[0], 0.0) / agreement[1]
    layers = []
    for shards in parts:
        gathered = []
        for order, s in zip(orders(nrep, ndp), shards):
            projected = (s[:, 0] - project_coef * s[:, 1]).astype(jnp.bfloat16)
            whole = gather_dp(projected, order, ndp)
            whole = whole.reshape((ndp,) + projected.shape).transpose(1, 0, 2, 3)
            gathered.append(whole.reshape(-1, projected.shape[-1]))
        layers.append(jnp.concatenate(gathered, axis=0))
    conv_grad = jnp.stack(layers).astype(jnp.float32)
    conv_square = conv_grad * conv_grad + eps_one
    conv_cols_new = decay_rate * conv_cols + (1.0 - decay_rate) * jnp.mean(conv_square, axis=1)
    row_part = jnp.sum(conv_square, axis=2)
    over_cols = jnp.sum(conv_grad * conv_grad / conv_cols_new[:, None, :], axis=2)
    weight_part = jnp.sum(conv_master * conv_master, axis=(1, 2))
    weight_part = jnp.broadcast_to(weight_part[:, None], (2, 128))
    row_pack = axis_sum(jnp.concatenate([row_part, over_cols, weight_part], axis=1), "rep")
    count = row_part.shape[1]
    row_total = row_pack[:, :count]
    over_total = row_pack[:, count : 2 * count]
    weight_total = row_pack[:, 2 * count]
    conv_rows_new = decay_rate * conv_rows + (1.0 - decay_rate) * row_total / channels
    row_mean = jnp.mean(conv_rows_new, axis=1)
    entries = conv_grad.shape[1] * channels
    update_rms = jnp.sqrt(row_mean * jnp.sum(over_total / conv_rows_new, axis=1) / entries)
    update = conv_grad * lax.rsqrt(
        conv_rows_new[:, :, None] * conv_cols_new[:, None, :] / row_mean[:, None, None]
    )
    update = update / jnp.maximum(1.0, update_rms / clip_level)[:, None, None]
    step_size = rel_step * jnp.maximum(eps_two, jnp.sqrt(weight_total / entries))
    conv_new = conv_master - step_size[:, None, None] * update
    head_grad = head_sum[0] - project_coef * head_sum[1]
    bias_grad = bias_sum[0] - project_coef * bias_sum[1]
    norm_grad = norm_both[0] - project_coef * norm_both[1]
    head_rows_new, head_cols_new, head_new = factored(
        head_master, head_grad, head_rows, head_cols, decay_rate
    )
    bias_moment_new, bias_new = plain(head_bias, bias_grad, head_bias_moment, decay_rate)
    norm_moment_new, norm_new = plain(
        jnp.stack([norm_gain, norm_bias]), norm_grad, norm_moment, decay_rate
    )
    cur_losses = jnp.stack([loss_sum[0], totals[1]])
    mem_losses = jnp.stack([loss_sum[1], totals[2]])
    return (
        cur_losses,
        mem_losses,
        agreement,
        conv_grad,
        conv_rows_new,
        conv_cols_new,
        conv_new,
        conv_new.astype(jnp.bfloat16),
        head_grad,
        head_rows_new,
        head_cols_new,
        head_new,
        head_new.astype(jnp.bfloat16),
        bias_grad,
        bias_moment_new,
        bias_new,
        norm_grad,
        norm_moment_new,
        norm_new,
    )


def solution(mesh):
    nrep = mesh.shape["rep"]
    ndp = mesh.shape["dp"]

    def run(*args):
        return local(nrep, ndp, *args)

    return jax.shard_map(
        run,
        mesh=mesh,
        in_specs=(
            P(("dp", "rep"), None, None, None),
            P(("dp", "rep")),
            P(("dp", "rep")),
            P(("dp", "rep")),
            P(("dp", "rep")),
            P(),
            P(None, None, "rep"),
            P(),
            P(None, "rep"),
            P(),
            P(),
            P(),
            P(),
            P(),
            P(),
            P(),
            P(),
        ),
        out_specs=(
            P(),
            P(),
            P(),
            P(None, None, "rep"),
            P(),
            P(None, "rep"),
            P(None, None, "rep"),
            P(None, None, "rep"),
            P(),
            P(),
            P(),
            P(),
            P(),
            P(),
            P(),
            P(),
            P(),
            P(),
            P(),
        ),
        check_vma=False,
    )
```

```python
import functools

import jax
import jax.numpy as jnp
from jax import lax
from jax.experimental import pallas as pl
from jax.experimental.pallas import tpu as pltpu
from jax.sharding import PartitionSpec as P

CLASSES = 10
TASKS = 10
STEP = 10


norm_eps = 1e-05
eps_one = 1e-30
eps_two = 0.001
rel_step = 0.5
clip_level = 1.0


def swap(x, axis, bit):
    n = lax.axis_size(axis)
    return lax.ppermute(x, axis, [(i, i ^ bit) for i in range(n)])


def bits_of(n):
    return [1 << k for k in range(n.bit_length() - 1)]


def exchange_sum(x, axis, basis):
    first = x + swap(x, axis, basis[0]) if len(basis) == 1 else None
    if first is not None:
        return first
    a, b = basis
    return (x + swap(x, axis, a)) + (swap(x, axis, b) + swap(x, axis, a ^ b))


def axis_sum(x, axis):
    bits = bits_of(lax.axis_size(axis))
    if len(bits) % 2:
        x = exchange_sum(x, axis, bits[:1])
        bits = bits[1:]
    while bits:
        x = exchange_sum(x, axis, bits[:2])
        bits = bits[2:]
    return x


def all_sum(x):
    return axis_sum(axis_sum(x, "rep"), "dp")


def coord(axis, bit):
    return (lax.axis_index(axis) & bit) // bit


def pick(x, dim, index):
    return lax.dynamic_index_in_dim(x, index, dim, keepdims=False)


def double(x, dim, axis, bit):
    other = swap(x, axis, bit)
    mine = coord(axis, bit) == 0
    return jnp.stack([jnp.where(mine, x, other), jnp.where(mine, other, x)], axis=dim)


def orders(nrep, ndp):
    rep_bits = [("rep", b) for b in bits_of(nrep)]
    dp_bits = [("dp", b) for b in bits_of(ndp)]
    core, rest = rep_bits[:1], rep_bits[1:]
    return [
        core + rest + dp_bits,
        core + dp_bits[:1] + rest + dp_bits[1:],
        core + dp_bits[1:] + dp_bits[:1] + rest,
    ]


def labels_of(nrep, ndp):
    return [("rep", b) for b in reversed(bits_of(nrep))] + [("dp", b) for b in reversed(bits_of(ndp))]


def gather_dp(x, order, ndp):
    target = [("dp", b) for b in reversed(bits_of(ndp))]
    names = []
    for key in reversed([k for k in order if k[0] == "dp"]):
        dim = sum(target.index(n) < target.index(key) for n in names)
        x = double(x, dim, *key)
        names.insert(dim, key)
    return x


bf16 = jnp.bfloat16
f32 = jnp.float32
MIB = 1 << 20


def params(mib, **more):
    return pltpu.CompilerParams(vmem_limit_bytes=mib * MIB, **more)


def whole(shape):
    return pl.BlockSpec(shape, lambda *_: (0,) * len(shape))


def scalars():
    return pl.BlockSpec(memory_space=pltpu.SMEM)


def middle_first(k):
    return jnp.where(k == 0, 1, jnp.where(k == 1, 0, 2))


def gate(v):
    return 0.5 + 0.5 * jnp.tanh(0.5 * v)


def norm_terms(stats, gain, norm_count):
    mean_val = stats[0:1] / norm_count
    rstd = lax.rsqrt(stats[1:2] / norm_count - mean_val * mean_val + norm_eps)
    return mean_val, rstd, rstd * gain


def conv_steps(cat, w_ref, live_ref, h_ref, stat_ref, side, rows):
    k = pl.program_id(0)
    wide = side * rows
    total = side * wide

    @pl.when(k == 0)
    def _():
        h_ref[...] = jnp.dot(cat[...], w_ref[...], preferred_element_type=f32)

    @pl.when(k == 1)
    def _():
        h_ref[wide:] += jnp.dot(cat[: total - wide], w_ref[...], preferred_element_type=f32)

    @pl.when(k == 2)
    def _():
        h_ref[: total - wide] += jnp.dot(cat[wide:], w_ref[...], preferred_element_type=f32)
        channels = h_ref.shape[1]

        def tile(i, sums):
            at = pl.multiple_of(i * 8, 8)
            mask = jnp.broadcast_to(live_ref[pl.ds(at, 8), :], (8, channels))
            one, two = sums
            for p in range(side * side):
                v = h_ref[pl.ds(p * rows + at, 8), :]
                m = v * mask
                one = one + m
                two = two + m * v
            return one, two

        zero = jnp.zeros((8, channels), f32)
        one, two = lax.fori_loop(0, rows // 8, tile, (zero, zero))
        stat_ref[0:1] = jnp.sum(one, axis=0, keepdims=True)
        stat_ref[1:2] = jnp.sum(two, axis=0, keepdims=True)


def put_shifted(cat, p, q, side, rows, channels, value):
    for kx in range(3):
        out_q = q - kx + 1
        if 0 <= out_q < side:
            at = (p * side + out_q) * rows
            cat[at : at + rows, kx * channels : (kx + 1) * channels] = value


def clear_edges(cat, p, side, rows, channels):
    zero = jnp.zeros((rows, channels), cat.dtype)
    at = p * side * rows
    cat[at : at + rows, :channels] = zero
    at = (p * side + side - 1) * rows
    cat[at : at + rows, 2 * channels :] = zero


def first_body(cat_ref, w_ref, live_ref, h_ref, stat_ref, *, side, rows):
    conv_steps(cat_ref, w_ref, live_ref, h_ref, stat_ref, side, rows)


def first_conv(cat, w, live, side):
    total, wide = cat.shape
    channels = w.shape[1]
    rows = total // (side * side)
    return pl.pallas_call(
        functools.partial(first_body, side=side, rows=rows),
        grid=(3,),
        in_specs=[
            whole(cat.shape),
            pl.BlockSpec((wide, channels), lambda k: (middle_first(k), 0)),
            whole(live.shape),
        ],
        out_specs=(whole((total, channels)), whole((2, channels))),
        out_shape=(
            jax.ShapeDtypeStruct((total, channels), f32),
            jax.ShapeDtypeStruct((2, channels), f32),
        ),
        compiler_params=params(24),
        cost_estimate=pl.CostEstimate(
            flops=6 * total * wide * channels, bytes_accessed=20 * MIB, transcendentals=0
        ),
        name="first_conv",
    )(cat, w, live)


def second_body(count_ref, h_in, stats_ref, gain_ref, bias_ref, w_ref, live_ref, cat_ref, h_ref, stat_ref, *, side, rows):
    channels = h_in.shape[1]

    @pl.when(pl.program_id(0) == 0)
    def _():
        mean_val, rstd, scale = norm_terms(stats_ref[...], gain_ref[...], count_ref[0])
        bias = bias_ref[...]
        for p in range(side):
            clear_edges(cat_ref, p, side, rows, channels)
            for q in range(side):
                at = (p * side + q) * rows
                pre = (h_in[at : at + rows] - mean_val) * scale + bias
                put_shifted(cat_ref, p, q, side, rows, channels, (pre * gate(pre)).astype(bf16))

    conv_steps(cat_ref, w_ref, live_ref, h_ref, stat_ref, side, rows)


def second_conv(count, h_in, stats, gain, bias, w, live, side):
    total, channels = h_in.shape
    wide = 3 * channels
    rows = total // (side * side)
    return pl.pallas_call(
        functools.partial(second_body, side=side, rows=rows),
        grid=(3,),
        in_specs=[
            scalars(),
            whole(h_in.shape),
            whole(stats.shape),
            whole(gain.shape),
            whole(bias.shape),
            pl.BlockSpec((wide, channels), lambda k: (middle_first(k), 0)),
            whole(live.shape),
        ],
        out_specs=(whole((total, wide)), whole((total, channels)), whole((2, channels))),
        out_shape=(
            jax.ShapeDtypeStruct((total, wide), bf16),
            jax.ShapeDtypeStruct((total, channels), f32),
            jax.ShapeDtypeStruct((2, channels), f32),
        ),
        compiler_params=params(32),
        cost_estimate=pl.CostEstimate(
            flops=6 * total * wide * channels, bytes_accessed=25 * MIB, transcendentals=total * channels
        ),
        name="second_conv",
    )(count, h_in, stats, gain, bias, w, live)


def head_body(
    count_ref,
    h_ref,
    x_ref,
    stats_ref,
    gain_ref,
    bias_ref,
    info_ref,
    head_ref,
    head_bias_ref,
    slope_ref,
    dpool_ref,
    sums_ref,
    part_ref,
    small_ref,
    pool_scr,
    slope_sum,
    normed_sum,
    *,
    area,
    classes,
):
    rows = info_ref.shape[0]
    channels = h_ref.shape[1]
    lanes = head_ref.shape[1]
    mean_val, rstd, _ = norm_terms(stats_ref[...], gain_ref[...], count_ref[0])
    gain = gain_ref[...]
    bias = bias_ref[...]

    def tile(i, _):
        at = pl.multiple_of(i * 16, 16)
        acc = jnp.zeros((16, channels), f32)
        acc_slope = jnp.zeros((16, channels), f32)
        acc_normed = jnp.zeros((16, channels), f32)
        for p in range(area):
            here = pl.ds(p * rows + at, 16)
            normed = (h_ref[here, :] - mean_val) * rstd
            joined = x_ref[here, :].astype(f32) + (normed * gain + bias)
            sig = gate(joined)
            out = joined * sig
            slope = sig * (1.0 + joined * (1.0 - sig))
            slope_ref[here, :] = slope
            acc = acc + out
            acc_slope = acc_slope + slope
            acc_normed = acc_normed + slope * normed
        pool_scr[pl.ds(at, 16), :] = (acc / area).astype(bf16)
        slope_sum[pl.ds(at, 16), :] = acc_slope
        normed_sum[pl.ds(at, 16), :] = acc_normed
        return 0

    lax.fori_loop(0, rows // 16, tile, 0)
    pooled = pool_scr[...]
    logits = jnp.dot(pooled, head_ref[...], preferred_element_type=f32) + head_bias_ref[...]
    lane = lax.broadcasted_iota(jnp.int32, (rows, lanes), 1).astype(f32)
    base = info_ref[:, 0:1]
    mask = (lane >= base) & (lane < base + classes)
    hot = (lane == info_ref[:, 1:2]).astype(f32)
    top = jnp.max(jnp.where(mask, logits, -jnp.inf), axis=1, keepdims=True)
    terms = jnp.where(mask, jnp.exp(jnp.where(mask, logits - top, 0.0)), 0.0)
    total = jnp.sum(terms, axis=1, keepdims=True)
    entropy = top + jnp.log(total) - jnp.sum(jnp.where(hot > 0.0, logits, 0.0), axis=1, keepdims=True)
    slant = terms / total - hot
    for o in range(2):
        weight = info_ref[:, 2 + o : 3 + o]
        dlogits = (slant * (weight * count_ref[1 + o])).astype(bf16)
        part_ref[:, o * lanes : (o + 1) * lanes] = lax.dot_general(
            pooled, dlogits, (((0,), (0,)), ((), ())), preferred_element_type=f32
        )
        small_ref[o : o + 1] = jnp.sum(dlogits.astype(f32), axis=0, keepdims=True)
        small_ref[2 + o : 3 + o] = jnp.broadcast_to(
            jnp.sum(weight * entropy, axis=0, keepdims=True), (1, lanes)
        )
        dpool = lax.dot_general(
            dlogits, head_ref[...], (((1,), (1,)), ((), ())), preferred_element_type=f32
        ) * (1.0 / area)
        dpool_ref[o] = dpool
        sums_ref[o : o + 1] = jnp.sum(dpool * slope_sum[...], axis=0, keepdims=True)
        sums_ref[2 + o : 3 + o] = jnp.sum(dpool * normed_sum[...], axis=0, keepdims=True)


def head_step(count, h, cat, stats, gain, bias, info, head, head_bias, area, classes):
    total, channels = h.shape
    rows = info.shape[0]
    lanes = head.shape[1]
    return pl.pallas_call(
        functools.partial(head_body, area=area, classes=classes),
        grid=(1,),
        in_specs=[
            scalars(),
            whole(h.shape),
            pl.BlockSpec((total, channels), lambda i: (0, 1)),
            whole(stats.shape),
            whole(gain.shape),
            whole(bias.shape),
            whole(info.shape),
            whole(head.shape),
            whole(head_bias.shape),
        ],
        out_specs=(
            whole((total, channels)),
            whole((2, rows, channels)),
            whole((4, channels)),
            whole((channels, 2 * lanes)),
            whole((4, lanes)),
        ),
        out_shape=(
            jax.ShapeDtypeStruct((total, channels), f32),
            jax.ShapeDtypeStruct((2, rows, channels), f32),
            jax.ShapeDtypeStruct((4, channels), f32),
            jax.ShapeDtypeStruct((channels, 2 * lanes), f32),
            jax.ShapeDtypeStruct((4, lanes), f32),
        ),
        scratch_shapes=[
            pltpu.VMEM((rows, channels), bf16),
            pltpu.VMEM((rows, channels), f32),
            pltpu.VMEM((rows, channels), f32),
        ],
        compiler_params=params(24),
        cost_estimate=pl.CostEstimate(
            flops=20 * total * channels, bytes_accessed=12 * MIB, transcendentals=total * channels
        ),
        name="head_step",
    )(count, h, cat, stats, gain, bias, info, head, head_bias)


def block_at(r, o, near, nrep):
    return pl.multiple_of((((r & 1) ^ near) * (nrep // 2) + r // 2) * 256 + o * 128, 128)


def back_two_body(near_ref, count_ref, slope_ref, dpool_ref, h_ref, stats_ref, gain_ref, sums_ref, live_ref, out_ref, *, area, nrep):
    rows = live_ref.shape[0]
    channels = h_ref.shape[1]
    near = near_ref[0]
    count = count_ref[0]
    mean_val, rstd, scale = norm_terms(stats_ref[...], gain_ref[...], count)
    for o in range(2):
        shift = sums_ref[o : o + 1] * scale / count
        gained = sums_ref[2 + o : 3 + o] * scale / count * rstd

        def tile(i, _):
            at = pl.multiple_of(i * 16, 16)
            mask = jnp.broadcast_to(live_ref[pl.ds(at, 16), :], (16, channels))
            lead = dpool_ref[o, pl.ds(at, 16), :] * scale
            offset = mask * shift
            factor = mask * gained
            for p in range(area):
                here = pl.ds(p * rows + at, 16)
                v = slope_ref[here, :] * lead - ((h_ref[here, :] - mean_val) * factor + offset)
                v = v.astype(bf16)
                for r in range(nrep):
                    out_ref[here, pl.ds(block_at(r, o, near, nrep), 128)] = v[:, r * 128 : (r + 1) * 128]
            return 0

        lax.fori_loop(0, rows // 16, tile, 0)


def back_two(near, count, slope, dpool, h, stats, gain, sums, live, area, nrep):
    total, channels = h.shape
    return pl.pallas_call(
        functools.partial(back_two_body, area=area, nrep=nrep),
        grid=(1,),
        in_specs=[scalars(), scalars()]
        + [whole(a.shape) for a in (slope, dpool, h, stats, gain, sums, live)],
        out_specs=whole((total, 2 * channels)),
        out_shape=jax.ShapeDtypeStruct((total, 2 * channels), bf16),
        compiler_params=params(24),
        cost_estimate=pl.CostEstimate(flops=16 * total * channels, bytes_accessed=10 * MIB, transcendentals=0),
        name="back_two",
    )(near, count, slope, dpool, h, stats, gain, sums, live)


def back_one_body(near_ref, count_ref, u_ref, h_ref, stats_ref, gain_ref, sums_ref, live_ref, out_ref, *, area, nrep):
    rows = live_ref.shape[0]
    channels = h_ref.shape[1]
    near = near_ref[0]
    count = count_ref[0]
    mean_val, rstd, scale = norm_terms(stats_ref[...], gain_ref[...], count)
    for o in range(2):
        shift = sums_ref[o : o + 1] * scale / count
        gained = sums_ref[2 + o : 3 + o] * scale / count * rstd

        def tile(i, _):
            at = pl.multiple_of(i * 16, 16)
            mask = jnp.broadcast_to(live_ref[pl.ds(at, 16), :], (16, channels))
            lead = mask * scale
            offset = mask * shift
            factor = mask * gained
            for p in range(area):
                here = pl.ds(p * rows + at, 16)
                v = u_ref[o, here, :] * lead - ((h_ref[here, :] - mean_val) * factor + offset)
                v = v.astype(bf16)
                for r in range(nrep):
                    out_ref[here, pl.ds(block_at(r, o, near, nrep), 128)] = v[:, r * 128 : (r + 1) * 128]
            return 0

        lax.fori_loop(0, rows // 16, tile, 0)


def back_one(near, count, u, h, stats, gain, sums, live, area, nrep):
    total, channels = h.shape
    return pl.pallas_call(
        functools.partial(back_one_body, area=area, nrep=nrep),
        grid=(1,),
        in_specs=[scalars(), scalars()]
        + [whole(a.shape) for a in (u, h, stats, gain, sums, live)],
        out_specs=whole((total, 2 * channels)),
        out_shape=jax.ShapeDtypeStruct((total, 2 * channels), bf16),
        compiler_params=params(32),
        cost_estimate=pl.CostEstimate(flops=16 * total * channels, bytes_accessed=13 * MIB, transcendentals=0),
        name="back_one",
    )(near, count, u, h, stats, gain, sums, live)


def weight_body(cat_ref, dh_ref, keep_ref, send_ref, *, ky, side, rows, nrep, ndp):
    wide = side * rows
    channels = dh_ref.shape[1] // 2
    lo, hi = (0, side - 1) if ky == 0 else ((0, side) if ky == 1 else (1, side))
    dlo = lo - (ky - 1)
    lhs = cat_ref[lo * wide : hi * wide]
    rhs = dh_ref[dlo * wide : (dlo + hi - lo) * wide]
    g = lax.dot_general(lhs, rhs, (((0,), (0,)), ((), ())), preferred_element_type=f32).astype(bf16)
    depth = channels // ndp
    for kx in range(3):
        for y in range(nrep // 2):
            for o in range(2):
                for ref, at in ((keep_ref, 0), (send_ref, channels)):
                    lane = at + y * 256 + o * 128
                    ref[y, :, kx, o] = g[
                        kx * channels : (kx + 1) * channels, lane : lane + 128
                    ].reshape(ndp, depth, 128)


def weight_grad(cat, dh, ky, side, nrep, ndp):
    total, wide = cat.shape
    channels = wide // 3
    shape = (nrep // 2, ndp, 3, 2, channels // ndp, 128)
    return pl.pallas_call(
        functools.partial(weight_body, ky=ky, side=side, rows=total // side**2, nrep=nrep, ndp=ndp),
        grid=(1,),
        in_specs=[whole(cat.shape), whole(dh.shape)],
        out_specs=(whole(shape), whole(shape)),
        out_shape=(jax.ShapeDtypeStruct(shape, bf16), jax.ShapeDtypeStruct(shape, bf16)),
        compiler_params=params(32),
        cost_estimate=pl.CostEstimate(flops=2 * total * wide * 2 * channels, bytes_accessed=12 * MIB, transcendentals=0),
        name=f"weight_grad_{ky}",
    )(cat, dh)


def act_body(near_ref, count_ref, dh_ref, w_ref, h_ref, stats_ref, gain_ref, bias_ref, out_ref, sums_ref, cat, *, side, nrep):
    o = pl.program_id(0)
    k = pl.program_id(1)
    total, channels = h_ref.shape
    rows = total // (side * side)
    wide = side * rows
    near = near_ref[0]

    @pl.when(k == 0)
    def _():
        for p in range(side):
            clear_edges(cat, p, side, rows, channels)
            for q in range(side):
                at = (p * side + q) * rows
                for r in range(nrep):
                    lane = block_at(r, 0, near, nrep) + o * 128
                    value = dh_ref[at : at + rows, pl.ds(pl.multiple_of(lane, 128), 128)]
                    for kx in range(3):
                        out_q = q + kx - 1
                        if 0 <= out_q < side:
                            to = (p * side + out_q) * rows
                            lane_to = (2 - kx) * channels + r * 128
                            cat[to : to + rows, lane_to : lane_to + 128] = value
        out_ref[0] = jnp.dot(cat[...], w_ref[...], preferred_element_type=f32)

    @pl.when(k == 1)
    def _():
        out_ref[0, : total - wide] += jnp.dot(cat[wide:], w_ref[...], preferred_element_type=f32)

    @pl.when(k == 2)
    def _():
        out_ref[0, wide:] += jnp.dot(cat[: total - wide], w_ref[...], preferred_element_type=f32)
        mean_val, rstd, _ = norm_terms(stats_ref[...], gain_ref[...], count_ref[0])
        gain = gain_ref[...]
        bias = bias_ref[...]

        def tile(i, sums):
            here = pl.ds(pl.multiple_of(i * 16, 16), 16)
            normed = (h_ref[here, :] - mean_val) * rstd
            pre = normed * gain + bias
            sig = gate(pre)
            v = out_ref[0, here, :] * (sig * (1.0 + pre * (1.0 - sig)))
            out_ref[0, here, :] = v
            return sums[0] + v, sums[1] + v * normed

        zero = jnp.zeros((16, channels), f32)
        one, two = lax.fori_loop(0, total // 16, tile, (zero, zero))
        sums_ref[0, 0:1] = jnp.sum(one, axis=0, keepdims=True)
        sums_ref[0, 1:2] = jnp.sum(two, axis=0, keepdims=True)


def act_grad(near, count, dh, w_turned, h, stats, gain, bias, side, nrep):
    total, channels = h.shape
    wide = 3 * channels
    return pl.pallas_call(
        functools.partial(act_body, side=side, nrep=nrep),
        grid=(2, 3),
        in_specs=[
            scalars(),
            scalars(),
            whole(dh.shape),
            pl.BlockSpec((wide, channels), lambda o, k: (middle_first(k), 0)),
            whole(h.shape),
            whole(stats.shape),
            whole(gain.shape),
            whole(bias.shape),
        ],
        out_specs=(
            pl.BlockSpec((1, total, channels), lambda o, k: (o, 0, 0)),
            pl.BlockSpec((1, 2, channels), lambda o, k: (o, 0, 0)),
        ),
        out_shape=(
            jax.ShapeDtypeStruct((2, total, channels), f32),
            jax.ShapeDtypeStruct((2, 2, channels), f32),
        ),
        scratch_shapes=[pltpu.VMEM((total, wide), bf16)],
        compiler_params=params(36),
        cost_estimate=pl.CostEstimate(
            flops=12 * total * wide * channels, bytes_accessed=20 * MIB, transcendentals=2 * total * channels
        ),
        name="act_grad",
    )(near, count, dh, w_turned, h, stats, gain, bias)


def weave_body(place_ref, own, near, half, other, straight, half_n, other_n, straight_n, *outs):
    t = pl.program_id(0)
    me = place_ref[0]
    mine = place_ref[1]
    out = outs[0]

    def put(block, value):
        out[:, pl.ds(pl.multiple_of(block * 128, 128), 128)] = value

    put(me, own[...])
    put(me ^ 1, near[...])
    for block, pieces in ((me ^ 2, (half, other, straight)), (me ^ 3, (half_n, other_n, straight_n))):
        for piece, when in zip(pieces, (t == mine, (t < 2) & (t != mine), t == 2)):

            @pl.when(when)
            def _(piece=piece, block=block):
                put(block, piece[...])

    if len(outs) > 1:
        channels = out.shape[1]
        for kx in range(3):
            outs[1][(2 - kx) * channels : (3 - kx) * channels, :] = out[
                kx * channels : (kx + 1) * channels, :
            ].T


def weave(place, pieces, turned):
    length, width = pieces[0].shape
    third = length // 3
    channels = 4 * width
    step = pl.BlockSpec((third, width), lambda t: (t, 0))
    whole_out = pl.BlockSpec((third, channels), lambda t: (t, 0))
    count = 2 if turned else 1
    return pl.pallas_call(
        weave_body,
        grid=(3,),
        in_specs=[scalars(), step, step] + [whole((third, width))] * 6,
        out_specs=(whole_out,) * count,
        out_shape=(jax.ShapeDtypeStruct((length, channels), bf16),) * count,
        compiler_params=params(20),
        cost_estimate=pl.CostEstimate(flops=0, bytes_accessed=4 * length * channels, transcendentals=0),
        name="weave",
    )(place, *pieces)


def dots_body(*refs):
    out = refs[-1]
    dot = jnp.zeros((1, 128), f32)
    square = jnp.zeros((1, 128), f32)
    for ref in refs[:-1]:
        for kx in range(ref.shape[0]):
            one = ref[kx, 0].astype(f32)
            two = ref[kx, 1].astype(f32)
            dot = dot + jnp.sum(one * two, axis=0, keepdims=True)
            square = square + jnp.sum(two * two, axis=0, keepdims=True)
    out[0:1] = dot
    out[1:2] = square


def dots(shards):
    return pl.pallas_call(
        dots_body,
        in_specs=[whole(x.shape) for x in shards],
        out_specs=whole((2, 128)),
        out_shape=jax.ShapeDtypeStruct((2, 128), f32),
        compiler_params=params(8),
        name="dots",
    )(*shards)


def project_body(coef_ref, *refs):
    count = len(refs) // 3
    coef = coef_ref[0]
    for i in range(count):
        for l in range(2):
            ref = refs[2 * i + l]
            for kx in range(ref.shape[0]):
                refs[2 * count + i][l, kx] = (
                    ref[kx, 0].astype(f32) - coef * ref[kx, 1].astype(f32)
                ).astype(bf16)


def project(coef, shards):
    count = len(shards) // 2
    shape = (2, shards[0].shape[0]) + shards[0].shape[2:]
    return pl.pallas_call(
        project_body,
        in_specs=[scalars()] + [whole(x.shape) for x in shards],
        out_specs=(whole(shape),) * count,
        out_shape=(jax.ShapeDtypeStruct(shape, bf16),) * count,
        compiler_params=params(8),
        name="project",
    )(coef, *shards)


def measure_body(cols_ref, *refs, decay, entries):
    *parts, grad_ref, cols_new_ref, rows_ref = refs
    l = pl.program_id(0)
    ndp, _, taps, depth, width = parts[0].shape
    span = taps * ndp * depth
    acc = jnp.zeros((1, width), f32)
    for i, part in enumerate(parts):
        for t in range(taps):
            v = part[:, 0, t].reshape(ndp * depth, width).astype(f32)
            at = i * span + t * ndp * depth
            grad_ref[0, at : at + ndp * depth] = v
            acc = acc + jnp.sum(v * v, axis=0, keepdims=True)
    cols_new = decay * cols_ref[0] + (1.0 - decay) * (acc / entries + eps_one)
    cols_new_ref[0] = cols_new
    weights = jnp.concatenate([jnp.ones((4, width), f32), jnp.broadcast_to(1.0 / cols_new, (4, width))], axis=0)
    for i in range(len(parts) * taps):
        at = i * ndp * depth
        v = grad_ref[0, at : at + ndp * depth]
        sums = lax.dot_general(
            weights, v * v, (((1,), (1,)), ((), ())), preferred_element_type=f32, precision=lax.Precision.HIGHEST
        )
        rows_ref[0, 0:1, at : at + ndp * depth] = sums[0:1]
        rows_ref[0, 1:2, at : at + ndp * depth] = sums[4:5]


def measure_rows(cols, parts, decay):
    ndp, layers, taps, depth, width = parts[0].shape
    length = len(parts) * taps * ndp * depth
    return pl.pallas_call(
        functools.partial(measure_body, decay=decay, entries=length),
        grid=(layers,),
        in_specs=[pl.BlockSpec((1, 1, width), lambda l: (l, 0, 0))]
        + [pl.BlockSpec((ndp, 1, taps, depth, width), lambda l: (0, l, 0, 0, 0))] * len(parts),
        out_specs=(
            pl.BlockSpec((1, length, width), lambda l: (l, 0, 0)),
            pl.BlockSpec((1, 1, width), lambda l: (l, 0, 0)),
            pl.BlockSpec((1, 2, length), lambda l: (l, 0, 0)),
        ),
        out_shape=(
            jax.ShapeDtypeStruct((layers, length, width), f32),
            jax.ShapeDtypeStruct((layers, 1, width), f32),
            jax.ShapeDtypeStruct((layers, 2, length), f32),
        ),
        compiler_params=params(24),
        cost_estimate=pl.CostEstimate(flops=0, bytes_accessed=12 * MIB, transcendentals=0),
        name="measure_rows",
    )(cols, *parts)


def update_body(grad_ref, master_ref, row_ref, col_ref, new_ref, copy_ref):
    factor = lax.dot_general(
        row_ref[0], col_ref[0], (((0,), (0,)), ((), ())), preferred_element_type=f32, precision=lax.Precision.HIGHEST
    )
    new = master_ref[0] - grad_ref[0] * factor
    new_ref[0] = new
    copy_ref[0] = new.astype(bf16)


def update(grad, master, row_factor, col_factor):
    layers, length, width = grad.shape
    step = length // 3
    block = pl.BlockSpec((1, step, width), lambda l, i: (l, i, 0))
    return pl.pallas_call(
        update_body,
        grid=(layers, 3),
        in_specs=[
            block,
            block,
            pl.BlockSpec((1, 1, step), lambda l, i: (l, 0, i)),
            pl.BlockSpec((1, 1, width), lambda l, i: (l, 0, 0)),
        ],
        out_specs=(block, block),
        out_shape=(
            jax.ShapeDtypeStruct((layers, length, width), f32),
            jax.ShapeDtypeStruct((layers, length, width), bf16),
        ),
        compiler_params=params(24),
        cost_estimate=pl.CostEstimate(flops=0, bytes_accessed=17 * MIB, transcendentals=0),
        name="update",
    )(grad, master, row_factor, col_factor)


def factored(weight, grad_mat, row_stat, col_stat, decay_rate):
    square = grad_mat * grad_mat + eps_one
    new_rows = decay_rate * row_stat + (1.0 - decay_rate) * jnp.mean(square, axis=-1)
    new_cols = decay_rate * col_stat + (1.0 - decay_rate) * jnp.mean(square, axis=-2)
    second_est = (
        new_rows[..., :, None]
        * new_cols[..., None, :]
        / jnp.mean(new_rows, axis=-1)[..., None, None]
    )
    update = grad_mat * lax.rsqrt(second_est)
    update = update / jnp.maximum(
        1.0, jnp.sqrt(jnp.mean(update * update, axis=(-2, -1), keepdims=True)) / clip_level
    )
    step_size = rel_step * jnp.maximum(
        eps_two, jnp.sqrt(jnp.mean(weight * weight, axis=(-2, -1), keepdims=True))
    )
    return (new_rows, new_cols, weight - step_size * update)


def plain(weight, grad_vec, moment, decay_rate):
    new_moment = decay_rate * moment + (1.0 - decay_rate) * (grad_vec * grad_vec + eps_one)
    update = grad_vec * lax.rsqrt(new_moment)
    update = update / jnp.maximum(
        1.0, jnp.sqrt(jnp.mean(update * update, axis=-1, keepdims=True)) / clip_level
    )
    step_size = rel_step * jnp.maximum(
        eps_two, jnp.sqrt(jnp.mean(weight * weight, axis=-1, keepdims=True))
    )
    return (new_moment, weight - step_size * update)


def after(first, second):
    return lax.optimization_barrier((first, second))


class Scatter:
    def __init__(self, keep, send, order, nrep, ndp):
        names = [key for key in labels_of(nrep, ndp) if key != order[0]]
        self.names = names
        self.order = order[1:]
        self.keep = keep.reshape(*[2] * len(names), *keep.shape[2:])
        self.send = send
        self.link = order[0]

    def go(self):
        self.recv = swap(self.send, *self.link).reshape(self.keep.shape)
        self.send = None

    def add(self):
        keep, recv = self.keep.astype(f32), self.recv.astype(f32)
        self.recv = None
        if not self.order:
            self.keep = (keep + recv).astype(bf16)
            return
        self.link, self.order = self.order[0], self.order[1:]
        dim = self.names.index(self.link)
        self.names = self.names[:dim] + self.names[dim + 1 :]
        mine = coord(*self.link)
        self.send = (pick(keep, dim, 1 - mine) + pick(recv, dim, 1 - mine)).astype(bf16)
        self.keep = (pick(keep, dim, mine) + pick(recv, dim, mine)).astype(bf16)


def layer_grad(cat, dh, side, nrep, ndp):
    tasks = []
    for ky, order in enumerate(orders(nrep, ndp)):
        task = Scatter(*weight_grad(cat, dh, ky, side, nrep, ndp), order, nrep, ndp)
        task.go()
        tasks.append(task)
    return tasks


def advance(tasks, held):
    for task in tasks:
        if task.recv is not None:
            task.add()
    busy = [task for task in tasks if task.send is not None]
    sends, held = after([task.send for task in busy], held)
    for task, send in zip(busy, sends):
        task.send = send
        task.go()
    return held


def finish(tasks):
    while any(task.recv is not None for task in tasks):
        for task in tasks:
            if task.recv is not None:
                task.add()
                if task.send is not None:
                    task.go()


def gather_start(lowered):
    third = lowered.shape[0] // 3
    mine = coord("dp", 1)
    near = swap(lowered, "rep", 1)
    half = swap(lax.dynamic_slice_in_dim(lowered, mine * third, third, 0), "rep", 2)
    straight = swap(lowered[2 * third :], "rep", 2)
    half_other = swap(half, "dp", 1)
    far = [half, half_other, straight]
    return [lowered, near] + far, [swap(x, "rep", 1) for x in far]


def all_sum_low(x):
    for axis in ("rep", "dp"):
        bits = bits_of(lax.axis_size(axis))
        while bits:
            take = len(bits) % 2 or 2
            low = x.astype(bf16)
            wide = lax.reduce_precision(x, 8, 7)
            parts = [swap(low, axis, b).astype(f32) for b in bits[:take]]
            if take == 1:
                x = wide + parts[0]
            else:
                x = (wide + parts[0]) + (parts[1] + swap(low, axis, bits[0] ^ bits[1]).astype(f32))
            bits = bits[take:]
    return x


def local(
    nrep,
    ndp,
    feats,
    labels,
    task_ids,
    live,
    branch,
    mem_counts,
    conv_master,
    conv_rows,
    conv_cols,
    head_master,
    head_rows,
    head_cols,
    head_bias,
    head_bias_moment,
    norm_gain,
    norm_bias,
    norm_moment,
):
    channels = feats.shape[3]
    map_side = feats.shape[1]
    area = map_side * map_side
    decay_rate = 1.0 - STEP ** (-0.8)
    live_rows = live.astype(jnp.float32)
    memory = branch.astype(jnp.float32)
    past_tasks = jnp.arange(TASKS - 1)
    inverse = jnp.sum(
        jnp.where(
            task_ids[:, None] == past_tasks[None, :],
            1.0 / mem_counts.astype(f32)[None, :],
            0.0,
        ),
        axis=1,
    )
    rows = feats.shape[0]
    cur_weight = live_rows * (1.0 - memory)
    mem_weight = live_rows * memory * inverse
    local_counts = jnp.stack([jnp.sum(live_rows), jnp.sum(cur_weight), jnp.sum(mem_weight)])
    near = coord("rep", 1).astype(jnp.int32).reshape(1)
    place = jnp.stack([lax.axis_index("rep"), coord("dp", 1)]).astype(jnp.int32)
    pieces_one, far_one = gather_start(conv_master[0].astype(bf16))
    lanes = TASKS * CLASSES + -TASKS * CLASSES % 128
    head_lowered = jnp.pad(head_master.astype(bf16), ((0, 0), (0, lanes - TASKS * CLASSES)))
    bias_row = jnp.pad(head_bias, (0, lanes - TASKS * CLASSES))[None]
    live_col = live_rows[:, None]
    base = (task_ids * CLASSES).astype(f32)
    info = jnp.stack([base, base + labels.astype(f32), cur_weight, mem_weight], axis=1)
    feats_pos = feats.transpose(1, 2, 0, 3)
    padded = jnp.pad(feats_pos, ((0, 0), (1, 1), (0, 0), (0, 0)))
    cat_one = jnp.concatenate([padded[:, kx : kx + map_side] for kx in range(3)], axis=3)
    cat_one = cat_one.reshape(area * rows, 3 * channels)
    (pieces_one, far_one), cat_one = after((pieces_one, far_one), cat_one)
    pieces_two, far_two = gather_start(after(conv_master[1].astype(bf16), pieces_one[2])[0])
    (kernel_one,) = weave(place, pieces_one + far_one, False)
    first_map, stats = first_conv(cat_one, kernel_one, live_col, map_side)
    (pieces_two, far_two, later_master), first_map = after((pieces_two, far_two, conv_master), first_map)
    kernel_two, turned = weave(place, pieces_two + far_two, True)
    weight_part = jnp.sum(later_master * later_master, axis=(1, 2))
    counts_row = jnp.pad(local_counts, (0, channels - 3))[None]
    packed = all_sum(jnp.concatenate([stats, counts_row], axis=0))
    stats_one = packed[:2]
    totals = packed[2, :3]
    norm_count = area * totals[0]
    count = jnp.stack([norm_count, 1.0 / totals[1], 1.0 / totals[2]])
    gain_row = [norm_gain[l : l + 1] for l in range(2)]
    shift_row = [norm_bias[l : l + 1] for l in range(2)]
    cat_two, second_map, stats_two = second_conv(
        count, first_map, stats_one, gain_row[0], shift_row[0], kernel_two, live_col, map_side
    )
    stats_two = all_sum(stats_two)
    slope, dpool, sums_two, head_part, small_part = head_step(
        count,
        second_map,
        cat_one,
        stats_two,
        gain_row[1],
        shift_row[1],
        info,
        head_lowered,
        bias_row,
        area,
        CLASSES,
    )
    sums_two = all_sum(sums_two)
    hidden_two = back_two(
        near, count, slope, dpool, second_map, stats_two, gain_row[1], sums_two, live_col, area, nrep
    )
    head_sums = [all_sum_low(head_part), all_sum(small_part)]
    scatter_two = layer_grad(cat_two, hidden_two, map_side, nrep, ndp)
    hidden_two = advance(scatter_two, hidden_two)
    upstream, sums_one = act_grad(
        near, count, hidden_two, turned, first_map, stats_one, gain_row[0], shift_row[0], map_side, nrep
    )
    sums_one = advance(scatter_two, sums_one)
    sums_one = all_sum(sums_one.transpose(1, 0, 2).reshape(4, channels))
    sums_one = advance(scatter_two, sums_one)
    hidden_one = back_one(
        near, count, upstream, first_map, stats_one, gain_row[0], sums_one, live_col, area, nrep
    )
    (head_pack, small_sum), hidden_one = after(head_sums, hidden_one)
    hidden_one = advance(scatter_two, hidden_one)
    scatter_one = layer_grad(cat_one, hidden_one, map_side, nrep, ndp)
    finish(scatter_two)
    finish(scatter_one)
    shards_one = [x.keep for x in scatter_one]
    shards_two = [x.keep for x in scatter_two]
    used = TASKS * CLASSES
    head_sum = jnp.stack([head_pack[:, :used], head_pack[:, lanes : lanes + used]])
    bias_sum = small_sum[:2, :used]
    loss_sum = small_sum[2:, 0]
    both = jnp.stack([sums_one.reshape(2, 2, channels), sums_two.reshape(2, 2, channels)], axis=2)
    norm_both = jnp.stack([both[1], both[0]], axis=1)
    small_dot = (
        jnp.sum(head_sum[0] * head_sum[1])
        + jnp.sum(bias_sum[0] * bias_sum[1])
        + jnp.sum(norm_both[0] * norm_both[1])
    )
    small_square = (
        jnp.sum(head_sum[1] * head_sum[1])
        + jnp.sum(bias_sum[1] * bias_sum[1])
        + jnp.sum(norm_both[1] * norm_both[1])
    )
    partial_value = dots(shards_one + shards_two)
    agreement = jnp.sum(all_sum(partial_value), axis=1) + jnp.stack([small_dot, small_square])
    project_coef = jnp.minimum(agreement[0], 0.0) / agreement[1]
    paired = [x for pair in zip(shards_one, shards_two) for x in pair]
    parts = [
        gather_dp(x, order, ndp).reshape((ndp,) + x.shape)
        for x, order in zip(project(project_coef.reshape(1), paired), orders(nrep, ndp))
    ]
    conv_grad, conv_cols_new, row_part = measure_rows(conv_cols[:, None], parts, decay_rate)
    conv_cols_new = conv_cols_new[:, 0]
    count_rows = conv_grad.shape[1]
    row_pack = jnp.concatenate([row_part.reshape(2, -1), jnp.broadcast_to(weight_part[:, None], (2, 128))], axis=1)
    row_pack = axis_sum(row_pack, "rep")
    row_total = row_pack[:, :count_rows]
    over_total = row_pack[:, count_rows : 2 * count_rows]
    weight_total = row_pack[:, 2 * count_rows]
    conv_rows_new = decay_rate * conv_rows + (1.0 - decay_rate) * (row_total / channels + eps_one)
    row_mean = jnp.mean(conv_rows_new, axis=1)
    entries = count_rows * channels
    update_rms = jnp.sqrt(row_mean * jnp.sum(over_total / conv_rows_new, axis=1) / entries)
    step_size = rel_step * jnp.maximum(eps_two, jnp.sqrt(weight_total / entries))
    step_size = step_size / jnp.maximum(1.0, update_rms / clip_level)
    row_factor = lax.rsqrt(conv_rows_new / row_mean[:, None])
    col_factor = lax.rsqrt(conv_cols_new) * step_size[:, None]
    conv_new, conv_copy_new = update(conv_grad, conv_master, row_factor[:, None], col_factor[:, None])
    head_grad = head_sum[0] - project_coef * head_sum[1]
    bias_grad = bias_sum[0] - project_coef * bias_sum[1]
    norm_grad = norm_both[0] - project_coef * norm_both[1]
    head_rows_new, head_cols_new, head_new = factored(
        head_master, head_grad, head_rows, head_cols, decay_rate
    )
    bias_moment_new, bias_new = plain(head_bias, bias_grad, head_bias_moment, decay_rate)
    norm_moment_new, norm_new = plain(
        jnp.stack([norm_gain, norm_bias]), norm_grad, norm_moment, decay_rate
    )
    cur_losses = jnp.stack([loss_sum[0], totals[1]])
    mem_losses = jnp.stack([loss_sum[1], totals[2]])
    return (
        cur_losses,
        mem_losses,
        agreement,
        conv_grad,
        conv_rows_new,
        conv_cols_new,
        conv_new,
        conv_copy_new,
        head_grad,
        head_rows_new,
        head_cols_new,
        head_new,
        head_new.astype(jnp.bfloat16),
        bias_grad,
        bias_moment_new,
        bias_new,
        norm_grad,
        norm_moment_new,
        norm_new,
    )


def solution(mesh):
    nrep = mesh.shape["rep"]
    ndp = mesh.shape["dp"]

    def run(*args):
        return local(nrep, ndp, *args)

    return jax.shard_map(
        run,
        mesh=mesh,
        in_specs=(
            P(("dp", "rep"), None, None, None),
            P(("dp", "rep")),
            P(("dp", "rep")),
            P(("dp", "rep")),
            P(("dp", "rep")),
            P(),
            P(None, None, "rep"),
            P(),
            P(None, "rep"),
            P(),
            P(),
            P(),
            P(),
            P(),
            P(),
            P(),
            P(),
        ),
        out_specs=(
            P(),
            P(),
            P(),
            P(None, None, "rep"),
            P(),
            P(None, "rep"),
            P(None, None, "rep"),
            P(None, None, "rep"),
            P(),
            P(),
            P(),
            P(),
            P(),
            P(),
            P(),
            P(),
            P(),
            P(),
            P(),
        ),
        check_vma=False,
    )
```

```python
import functools

import jax
import jax.numpy as jnp
from jax import lax
from jax.experimental import pallas as pl
from jax.experimental.pallas import tpu as pltpu
from jax.sharding import PartitionSpec as P

CLASSES = 10
TASKS = 10
STEP = 10


norm_eps = 1e-05
eps_one = 1e-30
eps_two = 0.001
rel_step = 0.5
clip_level = 1.0


def swap(x, axis, bit):
    n = lax.axis_size(axis)
    return lax.ppermute(x, axis, [(i, i ^ bit) for i in range(n)])


def bits_of(n):
    return [1 << k for k in range(n.bit_length() - 1)]


def exchange_sum(x, axis, basis):
    first = x + swap(x, axis, basis[0]) if len(basis) == 1 else None
    if first is not None:
        return first
    a, b = basis
    return (x + swap(x, axis, a)) + (swap(x, axis, b) + swap(x, axis, a ^ b))


def axis_sum(x, axis):
    bits = bits_of(lax.axis_size(axis))
    if len(bits) % 2:
        x = exchange_sum(x, axis, bits[:1])
        bits = bits[1:]
    while bits:
        x = exchange_sum(x, axis, bits[:2])
        bits = bits[2:]
    return x


def all_sum(x):
    return axis_sum(axis_sum(x, "rep"), "dp")


def exchange_far(x, ndp):
    bits = bits_of(ndp)[1:]
    while bits:
        x = exchange_sum(x, "dp", bits[:2])
        bits = bits[2:]
    return x


def exchange_near(x, ndp):
    return axis_sum(exchange_sum(x, "dp", bits_of(ndp)[:1]), "rep")


def coord(axis, bit):
    return (lax.axis_index(axis) & bit) // bit


def pick(x, dim, index):
    return lax.dynamic_index_in_dim(x, index, dim, keepdims=False)


def double(x, dim, axis, bit):
    other = swap(x, axis, bit)
    mine = coord(axis, bit) == 0
    return jnp.stack([jnp.where(mine, x, other), jnp.where(mine, other, x)], axis=dim)


def orders(nrep, ndp):
    rep_bits = [("rep", b) for b in bits_of(nrep)]
    dp_bits = [("dp", b) for b in bits_of(ndp)]
    core, rest = rep_bits[:1], rep_bits[1:]
    return [
        core + rest + dp_bits,
        core + dp_bits[:1] + rest + dp_bits[1:],
        core + dp_bits[1:2] + dp_bits[:1] + dp_bits[2:] + rest,
    ]


def labels_of(nrep, ndp):
    return [("rep", b) for b in reversed(bits_of(nrep))] + [("dp", b) for b in reversed(bits_of(ndp))]


def gather_dp(x, names, order, ndp):
    target = [("dp", b) for b in reversed(bits_of(ndp))]
    names = list(names)
    for key in order:
        dim = sum(target.index(n) < target.index(key) for n in names)
        x = double(x, dim, *key)
        names.insert(dim, key)
    return x


bf16 = jnp.bfloat16
f32 = jnp.float32
MIB = 1 << 20
SCALE = 0.01


def params(mib, **more):
    return pltpu.CompilerParams(vmem_limit_bytes=mib * MIB, **more)


def whole(shape):
    return pl.BlockSpec(shape, lambda *_: (0,) * len(shape))


def cost(us):
    return pl.CostEstimate(flops=int(us * SCALE * 1.1e9), bytes_accessed=1 << 16, transcendentals=0)


def in_hbm(x):
    return pltpu.with_memory_space_constraint(x, pltpu.HBM)


def scalars():
    return pl.BlockSpec(memory_space=pltpu.SMEM)


def middle_first(k):
    return jnp.where(k == 0, 1, jnp.where(k == 1, 0, 2))


def gate(v):
    return 0.5 + 0.5 * jnp.tanh(0.5 * v)


def norm_terms(stats_ref, first_ref, gain, area):
    count = first_ref[2:3, 0:1] * area
    mean_val = stats_ref[0:1] / count
    rstd = lax.rsqrt(stats_ref[1:2] / count - mean_val * mean_val + norm_eps)
    return mean_val, rstd, rstd * gain, count


def assemble(place_ref, t, pieces, out):
    me = place_ref[0]
    mine = place_ref[1]

    def put(block, ref):
        out[:, pl.ds(pl.multiple_of(block * 128, 128), 128)] = ref[...]

    put(me, pieces[0])
    put(me ^ 1, pieces[1])
    for i, when in enumerate((t == mine, (t < 2) & (t != mine), t == 2)):

        @pl.when(when)
        def _(i=i):
            put(me ^ 2, pieces[2 + i])
            put(me ^ 3, pieces[5 + i])


def piece_specs(pieces, row):
    length, width = pieces[0].shape
    third = length // 3
    step = pl.BlockSpec((third, width), lambda k: (row(k), 0))
    return [step if x.shape[0] == length else whole(x.shape) for x in pieces]


def conv_steps(cat, w_ref, live_ref, h_ref, stat_ref, side, rows, counts=None):
    k = pl.program_id(0)
    wide = side * rows
    total = side * wide

    @pl.when(k == 0)
    def _():
        h_ref[...] = jnp.dot(cat[...], w_ref[...], preferred_element_type=f32)

    @pl.when(k == 1)
    def _():
        h_ref[wide:] += jnp.dot(cat[: total - wide], w_ref[...], preferred_element_type=f32)

    @pl.when(k == 2)
    def _():
        h_ref[: total - wide] += jnp.dot(cat[wide:], w_ref[...], preferred_element_type=f32)
        channels = h_ref.shape[1]

        def tile(i, sums):
            at = pl.multiple_of(i * 8, 8)
            mask = jnp.broadcast_to(live_ref[pl.ds(at, 8), 4:5], (8, channels))
            one, two = sums
            for p in range(side * side):
                v = h_ref[pl.ds(p * rows + at, 8), :]
                m = v * mask
                one = one + m
                two = two + m * v
            return one, two

        zero = jnp.zeros((8, channels), f32)
        one, two = lax.fori_loop(0, rows // 8, tile, (zero, zero))
        stat_ref[0:1] = jnp.sum(one, axis=0, keepdims=True)
        stat_ref[1:2] = jnp.sum(two, axis=0, keepdims=True)
        stat_ref[2:8] = jnp.zeros((6, channels), f32)
        if counts is not None:
            stat_ref[2:3] = counts[...]


def put_shifted(cat, p, q, side, rows, channels, value):
    for kx in range(3):
        out_q = q - kx + 1
        if 0 <= out_q < side:
            at = (p * side + out_q) * rows
            cat[at : at + rows, kx * channels : (kx + 1) * channels] = value


def clear_edges(cat, p, side, rows, channels):
    zero = jnp.zeros((rows, channels), cat.dtype)
    at = p * side * rows
    cat[at : at + rows, :channels] = zero
    at = (p * side + side - 1) * rows
    cat[at : at + rows, 2 * channels :] = zero


def first_body(place_ref, cat_ref, live_ref, counts_ref, *refs, side, rows):
    pieces, h_ref, stat_ref, w = refs[:8], *refs[8:]
    assemble(place_ref, middle_first(pl.program_id(0)), pieces, w)
    conv_steps(cat_ref, w, live_ref, h_ref, stat_ref, side, rows, counts_ref)


def first_conv(place, cat, live, counts, *pieces, side):
    total, wide = cat.shape
    channels = wide // 3
    rows = total // (side * side)
    return pl.pallas_call(
        functools.partial(first_body, side=side, rows=rows),
        grid=(3,),
        in_specs=[scalars(), whole(cat.shape), whole(live.shape), whole(counts.shape)]
        + piece_specs(pieces, middle_first),
        out_specs=(whole((total, channels)), whole((8, channels))),
        out_shape=(
            jax.ShapeDtypeStruct((total, channels), f32),
            jax.ShapeDtypeStruct((8, channels), f32),
        ),
        scratch_shapes=[pltpu.VMEM((wide, channels), bf16)],
        compiler_params=params(32),
        cost_estimate=cost(9),
        name="first_conv",
    )(place, cat, live, counts, *pieces)


def second_body(place_ref, h_in, stats_ref, gain_ref, bias_ref, live_ref, *refs, side, rows):
    pieces, cat_ref, h_ref, stat_ref, normed_ref, w = refs[:8], *refs[8:]
    channels = h_in.shape[1]

    @pl.when(pl.program_id(0) == 0)
    def _():
        gain = gain_ref[0:1]
        bias = bias_ref[0:1]
        mean_val, rstd, _, _ = norm_terms(stats_ref, stats_ref, gain, side * side)
        for p in range(side):
            clear_edges(cat_ref, p, side, rows, channels)
            for q in range(side):
                at = (p * side + q) * rows
                normed = (h_in[at : at + rows] - mean_val) * rstd
                normed_ref[at : at + rows] = normed.astype(bf16)
                pre = normed * gain + bias
                put_shifted(cat_ref, p, q, side, rows, channels, (pre * gate(pre)).astype(bf16))

    assemble(place_ref, middle_first(pl.program_id(0)), pieces, w)
    conv_steps(cat_ref, w, live_ref, h_ref, stat_ref, side, rows)


def second_conv(place, h_in, stats, gain, bias, live, *pieces, side):
    total, channels = h_in.shape
    wide = 3 * channels
    rows = total // (side * side)
    return pl.pallas_call(
        functools.partial(second_body, side=side, rows=rows),
        grid=(3,),
        in_specs=[scalars()]
        + [whole(x.shape) for x in (h_in, stats, gain, bias, live)]
        + piece_specs(pieces, middle_first),
        out_specs=(
            whole((total, wide)),
            whole((total, channels)),
            whole((8, channels)),
            whole((total, channels)),
        ),
        out_shape=(
            jax.ShapeDtypeStruct((total, wide), bf16),
            jax.ShapeDtypeStruct((total, channels), f32),
            jax.ShapeDtypeStruct((8, channels), f32),
            jax.ShapeDtypeStruct((total, channels), bf16),
        ),
        scratch_shapes=[pltpu.VMEM((wide, channels), bf16)],
        compiler_params=params(40),
        cost_estimate=cost(10),
        name="second_conv",
    )(place, h_in, stats, gain, bias, live, *pieces)


def head_body(
    near_ref,
    h_ref,
    x_ref,
    stats_ref,
    first_ref,
    gain_ref,
    bias_ref,
    info_ref,
    head_ref,
    head_bias_ref,
    slope_ref,
    normed_ref,
    dpool_ref,
    sums_ref,
    send_ref,
    keep_ref,
    pool_scr,
    slope_sum,
    normed_sum,
    part,
    *,
    area,
    classes,
):
    rows = info_ref.shape[0]
    channels = h_ref.shape[1]
    lanes = head_ref.shape[1]
    gain = gain_ref[1:2]
    bias = bias_ref[1:2]
    mean_val, rstd, _, _ = norm_terms(stats_ref, first_ref, gain, area)

    def tile(i, _):
        at = pl.multiple_of(i * 16, 16)
        acc = jnp.zeros((16, channels), f32)
        acc_slope = jnp.zeros((16, channels), f32)
        acc_normed = jnp.zeros((16, channels), f32)
        for p in range(area):
            here = pl.ds(p * rows + at, 16)
            normed = (h_ref[here, :] - mean_val) * rstd
            joined = x_ref[here, :].astype(f32) + (normed * gain + bias)
            sig = gate(joined)
            out = joined * sig
            slope = sig * (1.0 + joined * (1.0 - sig))
            slope_ref[here, :] = slope.astype(bf16)
            normed_ref[here, :] = normed.astype(bf16)
            acc = acc + out
            acc_slope = acc_slope + slope
            acc_normed = acc_normed + slope * normed
        pool_scr[pl.ds(at, 16), :] = (acc / area).astype(bf16)
        slope_sum[pl.ds(at, 16), :] = acc_slope
        normed_sum[pl.ds(at, 16), :] = acc_normed
        return 0

    lax.fori_loop(0, rows // 16, tile, 0)
    pooled = pool_scr[...]
    logits = jnp.dot(pooled, head_ref[...], preferred_element_type=f32) + head_bias_ref[...]
    lane = lax.broadcasted_iota(jnp.int32, (rows, lanes), 1).astype(f32)
    base = info_ref[:, 0:1]
    mask = (lane >= base) & (lane < base + classes)
    hot = (lane == info_ref[:, 1:2]).astype(f32)
    top = jnp.max(jnp.where(mask, logits, -jnp.inf), axis=1, keepdims=True)
    terms = jnp.where(mask, jnp.exp(jnp.where(mask, logits - top, 0.0)), 0.0)
    total = jnp.sum(terms, axis=1, keepdims=True)
    entropy = top + jnp.log(total) - jnp.sum(jnp.where(hot > 0.0, logits, 0.0), axis=1, keepdims=True)
    slant = terms / total - hot
    both = 0.0
    for o in range(2):
        weight = info_ref[:, 2 + o : 3 + o]
        dlogits = slant * (weight * (1.0 / first_ref[2:3, 1 + o : 2 + o]))
        both = both + dlogits
        dlogits = dlogits.astype(bf16)
        sums_ref[4:5, o * lanes : (o + 1) * lanes] = jnp.sum(dlogits.astype(f32), axis=0, keepdims=True)
        sums_ref[4:5, (2 + o) * lanes : (3 + o) * lanes] = jnp.broadcast_to(
            jnp.sum(weight * entropy, axis=0, keepdims=True), (1, lanes)
        )
        dpool = lax.dot_general(
            dlogits, head_ref[...], (((1,), (1,)), ((), ())), preferred_element_type=f32
        ) * (1.0 / area)
        dpool_ref[o] = dpool
        sums_ref[o : o + 1] = jnp.sum(dpool * slope_sum[...], axis=0, keepdims=True)
        sums_ref[2 + o : 3 + o] = jnp.sum(dpool * normed_sum[...], axis=0, keepdims=True)
    sums_ref[5:8] = jnp.zeros((3, channels), f32)
    part[...] = lax.dot_general(
        pooled, both.astype(bf16), (((0,), (0,)), ((), ())), preferred_element_type=f32
    ).astype(bf16)
    half = channels // 2
    near = near_ref[0]
    keep_ref[...] = part[pl.ds(pl.multiple_of(near * half, half), half), :]
    send_ref[...] = part[pl.ds(pl.multiple_of((1 - near) * half, half), half), :]


def head_step(near, h, cat, stats, first, gain, bias, info, head, head_bias, area, classes):
    total, channels = h.shape
    rows = info.shape[0]
    lanes = head.shape[1]
    return pl.pallas_call(
        functools.partial(head_body, area=area, classes=classes),
        grid=(1,),
        in_specs=[
            scalars(),
            whole(h.shape),
            pl.BlockSpec((total, channels), lambda i: (0, 1)),
        ]
        + [whole(x.shape) for x in (stats, first, gain, bias, info, head, head_bias)],
        out_specs=(
            whole((total, channels)),
            whole((total, channels)),
            whole((2, rows, channels)),
            whole((8, channels)),
            whole((channels // 2, lanes)),
            whole((channels // 2, lanes)),
        ),
        out_shape=(
            jax.ShapeDtypeStruct((total, channels), bf16),
            jax.ShapeDtypeStruct((total, channels), bf16),
            jax.ShapeDtypeStruct((2, rows, channels), f32),
            jax.ShapeDtypeStruct((8, channels), f32),
            jax.ShapeDtypeStruct((channels // 2, lanes), bf16),
            jax.ShapeDtypeStruct((channels // 2, lanes), bf16),
        ),
        scratch_shapes=[
            pltpu.VMEM((rows, channels), bf16),
            pltpu.VMEM((rows, channels), f32),
            pltpu.VMEM((rows, channels), f32),
            pltpu.VMEM((channels, lanes), bf16),
        ],
        compiler_params=params(20),
        cost_estimate=cost(3),
        name="head_step",
    )(near, h, cat, stats, first, gain, bias, info, head, head_bias)


def head_join_body(mine_ref, x_ref, other_ref, out_ref):
    half = x_ref.shape[0]
    mine = mine_ref[0]
    out_ref[pl.ds(pl.multiple_of(mine * half, half), half), :] = x_ref[...]
    out_ref[pl.ds(pl.multiple_of((1 - mine) * half, half), half), :] = other_ref[...]


def head_join(mine, x, other):
    rows, lanes = x.shape
    return pl.pallas_call(
        head_join_body,
        in_specs=[scalars(), whole(x.shape), whole(x.shape)],
        out_specs=whole((2 * rows, lanes)),
        out_shape=jax.ShapeDtypeStruct((2 * rows, lanes), bf16),
        compiler_params=params(4),
        cost_estimate=cost(0.7),
        name="head_join",
    )(mine, x, other)


def head_split_body(mine_ref, keep_ref, recv_ref, send_out, keep_out):
    half = send_out.shape[0]
    mine = mine_ref[0]
    here = pl.ds(pl.multiple_of(mine * half, half), half)
    there = pl.ds(pl.multiple_of((1 - mine) * half, half), half)
    keep_out[...] = keep_ref[here, :] + recv_ref[here, :]
    send_out[...] = keep_ref[there, :] + recv_ref[there, :]


def head_split(mine, keep, recv):
    rows, lanes = keep.shape
    out = jax.ShapeDtypeStruct((rows // 2, lanes), bf16)
    return pl.pallas_call(
        head_split_body,
        in_specs=[scalars(), whole(keep.shape), whole(keep.shape)],
        out_specs=(whole(out.shape),) * 2,
        out_shape=(out, out),
        compiler_params=params(4),
        cost_estimate=cost(0.7),
        name="head_split",
    )(mine, keep, recv)


def block_at(r, o, near, nrep):
    return pl.multiple_of((((r & 1) ^ near) * (nrep // 2) + r // 2) * 256 + o * 128, 128)


def back_two_body(near_ref, slope_ref, dpool_ref, h_ref, stats_ref, first_ref, gain_ref, sums_ref, live_ref, out_ref, *, area, nrep):
    rows = live_ref.shape[0]
    channels = h_ref.shape[1]
    near = near_ref[0]
    _, _, scale, count = norm_terms(stats_ref, first_ref, gain_ref[1:2], area)
    for o in range(2):
        shift = sums_ref[o : o + 1] * scale / count
        gained = sums_ref[2 + o : 3 + o] * scale / count

        def tile(i, _):
            at = pl.multiple_of(i * 16, 16)
            mask = jnp.broadcast_to(live_ref[pl.ds(at, 16), 4:5], (16, channels))
            lead = dpool_ref[o, pl.ds(at, 16), :] * scale
            offset = mask * shift
            factor = mask * gained
            for p in range(area):
                here = pl.ds(p * rows + at, 16)
                v = slope_ref[here, :].astype(f32) * lead - (h_ref[here, :].astype(f32) * factor + offset)
                v = v.astype(bf16)
                for r in range(nrep):
                    out_ref[here, pl.ds(block_at(r, o, near, nrep), 128)] = v[:, r * 128 : (r + 1) * 128]
            return 0

        lax.fori_loop(0, rows // 16, tile, 0)


def back_two(near, slope, dpool, h, stats, first, gain, sums, live, area, nrep):
    total, channels = h.shape
    return pl.pallas_call(
        functools.partial(back_two_body, area=area, nrep=nrep),
        grid=(1,),
        in_specs=[scalars()]
        + [whole(a.shape) for a in (slope, dpool, h, stats, first, gain, sums, live)],
        out_specs=whole((total, 2 * channels)),
        out_shape=jax.ShapeDtypeStruct((total, 2 * channels), bf16),
        compiler_params=params(24),
        cost_estimate=cost(3),
        name="back_two",
    )(near, slope, dpool, h, stats, first, gain, sums, live)


def back_one_body(near_ref, u_one, u_two, h_ref, stats_ref, gain_ref, sums_ref, live_ref, out_ref, *, area, nrep):
    rows = live_ref.shape[0]
    channels = h_ref.shape[1]
    near = near_ref[0]
    _, _, scale, count = norm_terms(stats_ref, stats_ref, gain_ref[0:1], area)
    for o in range(2):
        shift = sums_ref[o : o + 1] * scale / count
        gained = sums_ref[2 + o : 3 + o] * scale / count

        def tile(i, _):
            at = pl.multiple_of(i * 16, 16)
            mask = jnp.broadcast_to(live_ref[pl.ds(at, 16), 4:5], (16, channels))
            lead = mask * scale
            offset = mask * shift
            factor = mask * gained
            for p in range(area):
                here = pl.ds(p * rows + at, 16)
                v = (u_one, u_two)[o][here, :].astype(f32) * lead - (h_ref[here, :].astype(f32) * factor + offset)
                v = v.astype(bf16)
                for r in range(nrep):
                    out_ref[here, pl.ds(block_at(r, o, near, nrep), 128)] = v[:, r * 128 : (r + 1) * 128]
            return 0

        lax.fori_loop(0, rows // 16, tile, 0)


def back_one(near, u_one, u_two, h, stats, gain, sums, live, area, nrep):
    total, channels = h.shape
    return pl.pallas_call(
        functools.partial(back_one_body, area=area, nrep=nrep),
        grid=(1,),
        in_specs=[scalars()]
        + [whole(a.shape) for a in (u_one, u_two, h, stats, gain, sums, live)],
        out_specs=whole((total, 2 * channels)),
        out_shape=jax.ShapeDtypeStruct((total, 2 * channels), bf16),
        compiler_params=params(32),
        cost_estimate=cost(3),
        name="back_one",
    )(near, u_one, u_two, h, stats, gain, sums, live)


def weight_body(cat_ref, dh_ref, *outs, kys, side, rows, nrep, ndp):
    wide = side * rows
    channels = dh_ref.shape[1] // 2
    depth = channels // ndp
    for i, ky in enumerate(kys):
        lo, hi = (0, side - 1) if ky == 0 else ((0, side) if ky == 1 else (1, side))
        dlo = lo - (ky - 1)
        lhs = cat_ref[lo * wide : hi * wide]
        rhs = dh_ref[dlo * wide : (dlo + hi - lo) * wide]
        g = lax.dot_general(lhs, rhs, (((0,), (0,)), ((), ())), preferred_element_type=f32).astype(bf16)
        for kx in range(3):
            for y in range(nrep // 2):
                for o in range(2):
                    for ref, at in ((outs[2 * i], 0), (outs[2 * i + 1], channels)):
                        lane = at + y * 256 + o * 128
                        ref[y, :, kx, o] = g[
                            kx * channels : (kx + 1) * channels, lane : lane + 128
                        ].reshape(ndp, depth, 128)


def weight_grad(cat, dh, kys, side, nrep, ndp):
    total, wide = cat.shape
    channels = wide // 3
    shape = (nrep // 2, ndp, 3, 2, channels // ndp, 128)
    count = 2 * len(kys)
    return pl.pallas_call(
        functools.partial(weight_body, kys=kys, side=side, rows=total // side**2, nrep=nrep, ndp=ndp),
        grid=(1,),
        in_specs=[whole(cat.shape), whole(dh.shape)],
        out_specs=(whole(shape),) * count,
        out_shape=(jax.ShapeDtypeStruct(shape, bf16),) * count,
        compiler_params=params(32),
        cost_estimate=cost(5 * len(kys)),
        name="weight_grad_" + "".join(map(str, kys)),
    )(cat, dh)


def act_body(near_ref, dh_ref, upper_ref, mid_ref, lower_ref, h_ref, gain_ref, bias_ref, *refs, side, nrep):
    *outs, sums_ref, cat, acc = refs
    total, channels = h_ref.shape
    rows = total // (side * side)
    wide = side * rows
    near = near_ref[0]
    gain = gain_ref[0:1]
    bias = bias_ref[0:1]
    for p in range(side):
        clear_edges(cat, p, side, rows, channels)
    sums_ref[4:8] = jnp.zeros((4, channels), f32)
    for o, out_ref in enumerate(outs):
        for p in range(side):
            for q in range(side):
                at = (p * side + q) * rows
                for r in range(nrep):
                    value = dh_ref[at : at + rows, pl.ds(block_at(r, o, near, nrep), 128)]
                    for kx in range(3):
                        out_q = q + kx - 1
                        if 0 <= out_q < side:
                            to = (p * side + out_q) * rows
                            lane_to = (2 - kx) * channels + r * 128
                            cat[to : to + rows, lane_to : lane_to + 128] = value
        acc[...] = jnp.dot(cat[...], mid_ref[...], preferred_element_type=f32)
        acc[: total - wide] += jnp.dot(cat[wide:], upper_ref[...], preferred_element_type=f32)
        acc[wide:] += jnp.dot(cat[: total - wide], lower_ref[...], preferred_element_type=f32)

        def tile(i, sums, out_ref=out_ref):
            here = pl.ds(pl.multiple_of(i * 16, 16), 16)
            normed = h_ref[here, :].astype(f32)
            pre = normed * gain + bias
            sig = gate(pre)
            v = acc[here, :] * (sig * (1.0 + pre * (1.0 - sig)))
            out_ref[here, :] = v.astype(bf16)
            return sums[0] + v, sums[1] + v * normed

        zero = jnp.zeros((16, channels), f32)
        one, two = lax.fori_loop(0, total // 16, tile, (zero, zero))
        sums_ref[o : o + 1] = jnp.sum(one, axis=0, keepdims=True)
        sums_ref[2 + o : 3 + o] = jnp.sum(two, axis=0, keepdims=True)


def act_grad(near, dh, upper, mid, low, h, gain, bias, side, nrep):
    total, channels = h.shape
    wide = 3 * channels
    operands = (dh, upper, mid, low, h, gain, bias)
    return pl.pallas_call(
        functools.partial(act_body, side=side, nrep=nrep),
        grid=(1,),
        in_specs=[scalars()] + [whole(x.shape) for x in operands],
        out_specs=(whole((total, channels)), whole((total, channels)), whole((8, channels))),
        out_shape=(
            jax.ShapeDtypeStruct((total, channels), bf16),
            jax.ShapeDtypeStruct((total, channels), bf16),
            jax.ShapeDtypeStruct((8, channels), f32),
        ),
        scratch_shapes=[pltpu.VMEM((total, wide), bf16), pltpu.VMEM((total, channels), f32)],
        compiler_params=params(24),
        cost_estimate=cost(20),
        name="act_grad",
    )(near, *operands)


def lower_body(master_ref, own_ref, straight_ref):
    low = master_ref[0].astype(bf16)
    own_ref[...] = low

    @pl.when(pl.program_id(0) == 2)
    def _():
        straight_ref[...] = low


def half_body(place_ref, master_ref, half_ref):
    half_ref[...] = master_ref[0].astype(bf16)


def lower_half(place, master, layer):
    length, width = master.shape[1:]
    third = length // 3
    return pl.pallas_call(
        half_body,
        grid_spec=pltpu.PrefetchScalarGridSpec(
            num_scalar_prefetch=1,
            grid=(1,),
            in_specs=[pl.BlockSpec((1, third, width), lambda i, at: (layer, at[1], 0))],
            out_specs=pl.BlockSpec((third, width), lambda i, at: (0, 0)),
        ),
        out_shape=pltpu.HBM((third, width), bf16),
        compiler_params=params(8),
        cost_estimate=cost(1),
        name="lower_half",
    )(place, in_hbm(master))


def lower(master, layer):
    length, width = master.shape[1:]
    third = length // 3
    return pl.pallas_call(
        lower_body,
        grid=(3,),
        in_specs=[pl.BlockSpec((1, third, width), lambda t: (layer, t, 0))],
        out_specs=(pl.BlockSpec((third, width), lambda t: (t, 0)), whole((third, width))),
        out_shape=(pltpu.HBM((length, width), bf16), pltpu.HBM((third, width), bf16)),
        compiler_params=params(8),
        cost_estimate=cost(3),
        name="lower",
    )(in_hbm(master))


def spread_body(x_ref, cat_ref, *, side, rows):
    channels = x_ref.shape[1]
    for p in range(side):
        clear_edges(cat_ref, p, side, rows, channels)
        for q in range(side):
            at = (p * side + q) * rows
            put_shifted(cat_ref, p, q, side, rows, channels, x_ref[at : at + rows])


def spread(x, side):
    total, channels = x.shape
    return pl.pallas_call(
        functools.partial(spread_body, side=side, rows=total // side**2),
        in_specs=[whole(x.shape)],
        out_specs=whole((total, 3 * channels)),
        out_shape=jax.ShapeDtypeStruct((total, 3 * channels), bf16),
        compiler_params=params(12),
        cost_estimate=cost(2),
        name="spread",
    )(x)


def merge_body(x_ref, *refs):
    *others, out = refs
    x = x_ref[...].astype(f32) + others[0][...].astype(f32)
    if len(others) == 3:
        x = x + (others[1][...].astype(f32) + others[2][...].astype(f32))
    out[...] = x.astype(out.dtype)


def merge(x, *others):
    return pl.pallas_call(
        merge_body,
        in_specs=[whole(x.shape)] * (1 + len(others)),
        out_specs=whole(x.shape),
        out_shape=jax.ShapeDtypeStruct(x.shape, x.dtype),
        compiler_params=params(4),
        cost_estimate=cost(0.7),
        name="merge",
    )(x, *others)


def split_body(mine_ref, keep_ref, recv_ref, send_out, keep_out):
    mine = mine_ref[0]
    for a in range(keep_ref.shape[0]):
        send_out[a] = keep_ref[a, 1 - mine] + recv_ref[a, 1 - mine]
        keep_out[a] = keep_ref[a, mine] + recv_ref[a, mine]


def split_sum(mine, keep, recv, outer):
    tail = keep.shape[-4:]
    rows = keep.size // (outer * 2 * tail[-1])
    shape = (outer, 2, rows, tail[-1])
    if outer >= 4:
        block = pl.BlockSpec((outer // 4, 2, rows, tail[-1]), lambda i: (i, 0, 0, 0))
        out_block = pl.BlockSpec((outer // 4, rows, tail[-1]), lambda i: (i, 0, 0))
        steps = 4
    else:
        steps = 4 if rows % 128 == 0 and rows >= 1024 else 1
        block = pl.BlockSpec((outer, 2, rows // steps, tail[-1]), lambda i: (0, 0, i, 0))
        out_block = pl.BlockSpec((outer, rows // steps, tail[-1]), lambda i: (0, i, 0))
    out = jax.ShapeDtypeStruct((outer, rows, tail[-1]), bf16)
    send, kept = pl.pallas_call(
        split_body,
        grid=(steps,),
        in_specs=[scalars(), block, block],
        out_specs=(out_block, out_block),
        out_shape=(out, out),
        compiler_params=params(8),
        cost_estimate=cost(1.5),
        name="split_sum",
    )(mine, keep.reshape(shape), recv.reshape(shape))
    lead = (-1,) + tail
    return send.reshape(lead), kept.reshape(lead)


def turn_body(place_ref, *refs, t):
    pieces, out, w = refs[:8], refs[8], refs[9]
    channels = out.shape[1]
    assemble(place_ref, t, pieces, w)
    for kx in range(3):
        out[(2 - kx) * channels : (3 - kx) * channels, :] = w[kx * channels : (kx + 1) * channels, :].T


def turn(place, *pieces, t):
    length, width = pieces[0].shape
    third = length // 3
    channels = 4 * width
    return pl.pallas_call(
        functools.partial(turn_body, t=t),
        grid=(1,),
        in_specs=[scalars()] + piece_specs(pieces, lambda k: t),
        out_specs=whole((third, channels)),
        out_shape=jax.ShapeDtypeStruct((third, channels), bf16),
        scratch_shapes=[pltpu.VMEM((third, channels), bf16)],
        compiler_params=params(12),
        cost_estimate=cost(2),
        name="turn",
    )(place, *pieces)


def small_body(one_ref, two_ref, head_ref, out_ref, *, border):
    dot = jnp.zeros((1, 128), f32)
    square = jnp.zeros((1, 128), f32)
    width = one_ref.shape[1] // 128
    for ref in (one_ref, two_ref):
        for kind in range(2):
            for j in range(width):
                lane = slice(j * 128, (j + 1) * 128)
                a = ref[2 * kind : 2 * kind + 1, lane]
                b = ref[2 * kind + 1 : 2 * kind + 2, lane]
                dot = dot + a * b
                square = square + b * b
    a = two_ref[4:5, 0:128]
    b = two_ref[4:5, 128:256]
    dot = dot + a * b
    square = square + b * b
    head = head_ref[...].astype(f32)
    lane = lax.broadcasted_iota(jnp.int32, head.shape, 1)
    head = jnp.where(lane < border, head, 0.0)
    square = square + jnp.sum(head * head, axis=0, keepdims=True)
    out_ref[0:1] = dot
    out_ref[1:2] = square


def small_dots(one, two, head, border):
    return pl.pallas_call(
        functools.partial(small_body, border=border),
        in_specs=[whole(one.shape), whole(two.shape), whole(head.shape)],
        out_specs=whole((2, 128)),
        out_shape=jax.ShapeDtypeStruct((2, 128), f32),
        compiler_params=params(4),
        cost_estimate=cost(1),
        name="small_dots",
    )(one, two, head)


def dots_body(*refs):
    count = (len(refs) - 1) // 3
    out = refs[-1]
    dot = jnp.zeros((1, 128), f32)
    square = jnp.zeros((1, 128), f32)
    for keep, recv, share in zip(refs[:count], refs[count : 2 * count], refs[2 * count : -1]):
        share[...] = keep[...] + recv[...]
        for kx in range(keep.shape[1]):
            one = share[0, kx, 0].astype(f32)
            two = share[0, kx, 1].astype(f32)
            dot = dot + jnp.sum(one * two, axis=0, keepdims=True)
            square = square + jnp.sum(two * two, axis=0, keepdims=True)
    out[0:1] = dot
    out[1:2] = square


def dots(*both):
    kept = both[: len(both) // 2]
    share = jax.ShapeDtypeStruct(kept[0].shape, bf16)
    return pl.pallas_call(
        dots_body,
        in_specs=[whole(x.shape) for x in both],
        out_specs=(whole(kept[0].shape),) * len(kept) + (whole((2, 128)),),
        out_shape=(share,) * len(kept) + (jax.ShapeDtypeStruct((2, 128), f32),),
        compiler_params=params(8),
        cost_estimate=cost(1),
        name="dots",
    )(*both)


def project_body(coef_ref, *refs):
    *shares, out = refs
    coef = coef_ref[0]
    for i, ref in enumerate(shares):
        taps = ref.shape[1]
        for t in range(taps):
            out[i * taps + t] = (ref[0, t, 0].astype(f32) - coef * ref[0, t, 1].astype(f32)).astype(bf16)


def project(coef, *shares):
    first = shares[0]
    shape = (len(shares) * first.shape[1],) + first.shape[3:]
    return pl.pallas_call(
        project_body,
        in_specs=[scalars()] + [whole(x.shape) for x in shares],
        out_specs=whole(shape),
        out_shape=jax.ShapeDtypeStruct(shape, bf16),
        compiler_params=params(8),
        cost_estimate=cost(1),
        name="project",
    )(coef, *shares)


def squares_body(master_ref, out_ref):
    @pl.when((pl.program_id(0) == 0) & (pl.program_id(1) == 0))
    def _():
        out_ref[...] = jnp.zeros_like(out_ref)

    v = master_ref[0]
    total = jnp.sum(jnp.sum(v * v, axis=0, keepdims=True), axis=1, keepdims=True)
    row = lax.broadcasted_iota(jnp.int32, out_ref.shape, 0)
    out_ref[...] += jnp.where(row == pl.program_id(0), total, 0.0)


def weight_squares(master):
    layers, length, width = master.shape
    return pl.pallas_call(
        squares_body,
        grid=(layers, 3),
        in_specs=[pl.BlockSpec((1, length // 3, width), lambda l, i: (l, i, 0))],
        out_specs=whole((layers, 128)),
        out_shape=jax.ShapeDtypeStruct((layers, 128), f32),
        compiler_params=params(8),
        cost_estimate=cost(4),
        name="weight_squares",
    )(in_hbm(master))


def small_update_body(
    coef_ref,
    head_ref,
    one_ref,
    two_ref,
    master_ref,
    rows_ref,
    cols_ref,
    bias_ref,
    bias_moment_ref,
    gain_ref,
    shift_ref,
    moment_ref,
    grad_out,
    rows_out,
    cols_out,
    new_out,
    copy_out,
    bias_grad_out,
    bias_moment_out,
    bias_out,
    norm_grad_out,
    norm_moment_out,
    norm_out,
    losses_out,
    *,
    decay,
    border,
):
    coef = coef_ref[0]
    channels, used = master_ref.shape

    def mean(v):
        return jnp.sum(jnp.sum(v, axis=0, keepdims=True), axis=1, keepdims=True) / v.size

    def step_of(weight):
        return rel_step * jnp.maximum(eps_two, jnp.sqrt(mean(weight * weight)))

    def clipped(u):
        return u / jnp.maximum(1.0, jnp.sqrt(mean(u * u)) / clip_level)

    head = head_ref[:, :used].astype(f32)
    lane = lax.broadcasted_iota(jnp.int32, head.shape, 1)
    grad = jnp.where(lane >= border, head, -coef * head)
    grad_out[...] = grad
    square = grad * grad
    row_sum = lax.dot_general(
        jnp.ones((8, used), f32), square, (((1,), (1,)), ((), ())), preferred_element_type=f32, precision=lax.Precision.HIGHEST
    )[0:1]
    rows_new = decay * rows_ref[...] + (1.0 - decay) * (row_sum / used + eps_one)
    cols_new = decay * cols_ref[...] + (1.0 - decay) * (jnp.sum(square, axis=0, keepdims=True) / channels + eps_one)
    rows_out[...] = rows_new
    cols_out[...] = cols_new
    factor = lax.dot_general(
        lax.rsqrt(rows_new / mean(rows_new)),
        lax.rsqrt(cols_new),
        (((0,), (0,)), ((), ())),
        preferred_element_type=f32,
        precision=lax.Precision.HIGHEST,
    )
    weight = master_ref[...]
    new = weight - step_of(weight) * clipped(grad * factor)
    new_out[...] = new
    copy_out[...] = new.astype(bf16)

    def plain(weight, grad, moment):
        moment = decay * moment + (1.0 - decay) * (grad * grad + eps_one)
        return moment, weight - step_of(weight) * clipped(grad * lax.rsqrt(moment))

    lanes = head_ref.shape[1]
    grad = two_ref[4:5, 0:used] - coef * two_ref[4:5, lanes : lanes + used]
    bias_grad_out[...] = grad
    bias_moment_out[...], bias_out[...] = plain(bias_ref[...], grad, bias_moment_ref[...])
    for kind, (at, vectors) in enumerate(((2, gain_ref), (0, shift_ref))):
        for layer, sums in enumerate((one_ref, two_ref)):
            row = slice(2 * kind + layer, 2 * kind + layer + 1)
            grad = sums[at : at + 1] - coef * sums[at + 1 : at + 2]
            norm_grad_out[row] = grad
            norm_moment_out[row], norm_out[row] = plain(vectors[layer : layer + 1], grad, moment_ref[row])
    losses_out[0:1] = two_ref[4:5, 2 * lanes : 3 * lanes]
    losses_out[1:2] = two_ref[4:5, 3 * lanes : 4 * lanes]


def small_update(coef, head, one, two, master, rows, cols, bias, bias_moment, gain, shift, moment, decay):
    operands = (head, one, two, master, rows, cols, bias, bias_moment, gain, shift, moment)
    outs = [(master.shape, f32), (rows.shape, f32), (cols.shape, f32), (master.shape, f32), (master.shape, bf16)]
    outs += [(bias.shape, f32)] * 3 + [(moment.shape, f32)] * 3 + [((2, 128), f32)]
    return pl.pallas_call(
        functools.partial(small_update_body, decay=decay, border=(TASKS - 1) * CLASSES),
        in_specs=[scalars()] + [whole(x.shape) for x in operands],
        out_specs=tuple(whole(shape) for shape, _ in outs),
        out_shape=tuple(jax.ShapeDtypeStruct(shape, dtype) for shape, dtype in outs),
        compiler_params=params(12),
        cost_estimate=cost(4),
        name="small_update",
    )(coef, *operands)


def measure_body(cols_ref, *refs, decay):
    *parts, cols_new_ref, rows_ref = refs
    for l, part_ref in enumerate(parts):
        ndp, taps, depth, width = part_ref.shape
        span = ndp * depth
        acc = jnp.zeros((1, width), f32)
        for t in range(taps):
            v = part_ref[:, t].reshape(span, width).astype(f32)
            acc = acc + jnp.sum(v * v, axis=0, keepdims=True)
        cols_new = decay * cols_ref[l : l + 1] + (1.0 - decay) * (acc / (taps * span) + eps_one)
        cols_new_ref[l : l + 1] = cols_new
        weights = jnp.concatenate(
            [jnp.ones((4, width), f32), jnp.broadcast_to(1.0 / cols_new, (4, width))], axis=0
        )
        for t in range(taps):
            v = part_ref[:, t].reshape(span, width).astype(f32)
            sums = lax.dot_general(
                weights, v * v, (((1,), (1,)), ((), ())), preferred_element_type=f32, precision=lax.Precision.HIGHEST
            )
            rows_ref[l, 0:1, t * span : (t + 1) * span] = sums[0:1]
            rows_ref[l, 1:2, t * span : (t + 1) * span] = sums[4:5]


def measure_rows(cols, *parts, decay):
    ndp, taps, depth, width = parts[0].shape
    length = taps * ndp * depth
    layers = len(parts)
    return pl.pallas_call(
        functools.partial(measure_body, decay=decay),
        in_specs=[whole(cols.shape)] + [whole(x.shape) for x in parts],
        out_specs=(whole((layers, width)), whole((layers, 2, length))),
        out_shape=(
            jax.ShapeDtypeStruct((layers, width), f32),
            jax.ShapeDtypeStruct((layers, 2, length), f32),
        ),
        compiler_params=params(12),
        cost_estimate=cost(3),
        name="measure_rows",
    )(cols, *parts)


def update_body(master_ref, row_ref, col_ref, *refs):
    *parts, grad_ref, new_ref, copy_ref = refs
    layer = pl.program_id(0)
    for l, part in enumerate(parts):

        @pl.when(layer == l)
        def _(part=part):
            ndp, taps, depth, width = part.shape
            for t in range(taps):
                grad_ref[0, t * ndp * depth : (t + 1) * ndp * depth] = (
                    part[:, t].reshape(ndp * depth, width).astype(f32)
                )

    factor = lax.dot_general(
        row_ref[0], col_ref[0], (((0,), (0,)), ((), ())), preferred_element_type=f32, precision=lax.Precision.HIGHEST
    )
    new = master_ref[0] - grad_ref[0] * factor
    new_ref[0] = new
    copy_ref[0] = new.astype(bf16)


def update(master, row_factor, col_factor, *parts):
    layers, length, width = master.shape
    ndp, taps, depth, _ = parts[0].shape
    steps = 3
    step = length // steps
    block = pl.BlockSpec((1, step, width), lambda l, i: (l, i, 0))
    part_block = pl.BlockSpec((ndp, taps // steps, depth, width), lambda l, i: (0, i, 0, 0))
    return pl.pallas_call(
        update_body,
        grid=(layers, steps),
        in_specs=[
            block,
            pl.BlockSpec((1, 1, step), lambda l, i: (l, 0, i)),
            pl.BlockSpec((1, 1, width), lambda l, i: (l, 0, 0)),
        ]
        + [part_block] * layers,
        out_specs=(block, block, block),
        out_shape=(
            jax.ShapeDtypeStruct((layers, length, width), f32),
            jax.ShapeDtypeStruct((layers, length, width), f32),
            jax.ShapeDtypeStruct((layers, length, width), bf16),
        ),
        compiler_params=params(24),
        cost_estimate=cost(8),
        name="update",
    )(in_hbm(master), row_factor, col_factor, *parts)


def after(first, second):
    return lax.optimization_barrier((first, second))


def low_sum(a, b):
    return (a.astype(f32) + b.astype(f32)).astype(bf16)


class Box:
    def __init__(self, value):
        self.value = value


class Chain:
    def __init__(self):
        self.last = []

    def run(self, step, *inputs):
        values = [x.value if isinstance(x, Box) else x for x in inputs]
        if self.last:
            held, values = after([box.value for box in self.last], values)
            for box, value in zip(self.last, held):
                box.value = value
        outs = step(*values)
        self.last = [Box(x) for x in (outs if isinstance(outs, (tuple, list)) else (outs,))]
        return self.last


class Sum:
    def __init__(self, chain, x, groups=None):
        self.chain = chain
        self.x = x
        if groups is None:
            groups = [("rep", bits_of(lax.axis_size("rep"))[:2])]
            groups += [("rep", [b]) for b in bits_of(lax.axis_size("rep"))[2:]]
            bits = bits_of(lax.axis_size("dp"))
            if len(bits) % 2:
                groups.append(("dp", bits[:1]))
                bits = bits[1:]
            while bits:
                groups.append(("dp", bits[:2]))
                bits = bits[2:]
        self.groups = groups
        self.go()

    def go(self):
        if not self.groups:
            return
        axis, bits = self.groups.pop(0)
        if len(bits) == 2:
            bits = [bits[0], bits[1], bits[0] ^ bits[1]]
        value = self.x.value
        with jax.named_scope(f"sum_{axis}{bits[0]}"):
            self.others = [swap(value, axis, b) for b in bits]

    def hop(self):
        (self.x,) = self.chain.run(merge, self.x, *self.others)
        self.others = None
        self.go()

    def finish(self):
        while self.others:
            self.hop()
        return self.x


class Scatter:
    def __init__(self, chain, keep, send, order, nrep, ndp, title):
        self.chain = chain
        self.names = [key for key in labels_of(nrep, ndp) if key != order[0]]
        self.order = list(order)
        self.keep = keep
        self.title = title
        self.tail = keep.value.shape[2:]
        self.go(send.value)

    def go(self, send):
        axis, bit = self.order.pop(0)
        with jax.named_scope(f"{self.title}_{axis}{bit}"):
            self.recv = swap(send, axis, bit)

    def step_late(self):
        axis, bit = self.order[0]
        dim = self.names.index(self.order[0])
        self.names.pop(dim)
        mine = coord(axis, bit)
        tail = self.keep.value.shape[-4:]

        def run(keep, recv):
            keep = keep.reshape((1 << dim, 2, -1) + tail)
            recv = recv.reshape(keep.shape)
            return (
                low_sum(pick(keep, 1, 1 - mine), pick(recv, 1, 1 - mine)).reshape((-1,) + tail),
                low_sum(pick(keep, 1, mine), pick(recv, 1, mine)).reshape((-1,) + tail),
            )

        send, self.keep = self.chain.run(run, self.keep, self.recv)
        self.go(send.value)

    def step(self):
        dim = self.names.index(self.order[0])
        self.names.pop(dim)
        mine = coord(*self.order[0]).astype(jnp.int32).reshape(1)
        outer = 1 << dim
        run = functools.partial(split_sum, outer=outer)
        send, self.keep = self.chain.run(run, mine, self.keep, self.recv)
        self.go(send.value)


def start_grads(chain, title, cat, dh, kys, side, nrep, ndp):
    outs = chain.run(functools.partial(weight_grad, kys=kys, side=side, nrep=nrep, ndp=ndp), cat, dh)
    return [
        Scatter(chain, outs[2 * i], outs[2 * i + 1], orders(nrep, ndp)[ky], nrep, ndp, f"{title}{ky}")
        for i, ky in enumerate(kys)
    ]


def far_pieces(half, other, straight):
    far = [half, other, straight]
    return far + [swap(x, "rep", 1) for x in far]


def local(
    nrep,
    ndp,
    feats,
    labels,
    task_ids,
    live,
    branch,
    mem_counts,
    conv_master,
    conv_rows,
    conv_cols,
    head_master,
    head_rows,
    head_cols,
    head_bias,
    head_bias_moment,
    norm_gain,
    norm_bias,
    norm_moment,
):
    channels = feats.shape[3]
    map_side = feats.shape[1]
    area = map_side * map_side
    decay_rate = 1.0 - STEP ** (-0.8)
    live_rows = live.astype(jnp.float32)
    memory = branch.astype(jnp.float32)
    past_tasks = jnp.arange(TASKS - 1)
    inverse = jnp.sum(
        jnp.where(
            task_ids[:, None] == past_tasks[None, :],
            1.0 / mem_counts.astype(f32)[None, :],
            0.0,
        ),
        axis=1,
    )
    rows = feats.shape[0]
    cur_weight = live_rows * (1.0 - memory)
    mem_weight = live_rows * memory * inverse
    local_counts = jnp.stack([jnp.sum(live_rows), jnp.sum(cur_weight), jnp.sum(mem_weight)])
    place = jnp.stack([lax.axis_index("rep"), coord("dp", 1)]).astype(jnp.int32)
    near = coord("rep", 1).astype(jnp.int32).reshape(1)
    far_side = coord("rep", 2).astype(jnp.int32).reshape(1)
    chain = Chain()
    half = lower_half(place, conv_master, 0)
    half_one = swap(half, "rep", 2)
    master, half = after(conv_master, half)
    lanes = TASKS * CLASSES + -TASKS * CLASSES % 128
    head_lowered = jnp.pad(head_master.astype(bf16), ((0, 0), (0, lanes - TASKS * CLASSES)))
    bias_row = jnp.pad(head_bias, (0, lanes - TASKS * CLASSES))[None]
    base = (task_ids * CLASSES).astype(f32)
    info = jnp.stack([base, base + labels.astype(f32), cur_weight, mem_weight, live_rows], axis=1)
    info = jnp.pad(info, ((0, 0), (0, 123)))
    feats_pos = feats.transpose(1, 2, 0, 3)
    feats_pos = feats_pos.reshape(area * rows, channels)
    counts_row = jnp.pad(local_counts, (0, channels - 3))[None]
    early = (info, counts_row, head_lowered, bias_row, near, far_side)
    (feats_pos, early), master = after((feats_pos, early), master)
    info, counts_row, head_lowered, bias_row, near, far_side = early
    own, straight = lower(master, 0)
    straight_one = swap(straight, "rep", 2)
    near_one = swap(own, "rep", 1)
    (half_one, own), feats_pos = after((half_one, own), feats_pos)
    other_one = swap(half_one, "dp", 1)
    cat_one = spread(feats_pos, map_side)
    master, cat_one = after(conv_master, cat_one)
    half_two = lower_half(place, master, 1)
    own_two, straight_two = lower(master, 1)
    (half_two, own_two, straight_two), straight_one = after((half_two, own_two, straight_two), straight_one)
    half_two = swap(half_two, "rep", 2)
    straight_two = swap(straight_two, "rep", 2)
    near_two = swap(own_two, "rep", 1)
    (cat_one, own), own_two = after((cat_one, own), own_two)
    first_map, stats = chain.run(
        functools.partial(first_conv, side=map_side),
        place, cat_one, info, counts_row, own, near_one, *far_pieces(half_one, other_one, straight_one),
    )
    first_map.value, half_two = after(first_map.value, half_two)
    other_two = swap(half_two, "dp", 1)
    stats_one = Sum(chain, stats)
    stats_one.hop()
    stats_one.hop()
    far_two = (half_two, other_two, straight_two)
    far_two, stats_one.x.value = after(far_two, stats_one.x.value)
    pieces_two = [own_two, near_two] + far_pieces(*far_two)
    stats_one = stats_one.finish()
    cat_two, second_map, stats, normed_one = chain.run(
        functools.partial(second_conv, side=map_side),
        place, first_map, stats_one, norm_gain, norm_bias, info, *pieces_two,
    )
    stats = Sum(chain, stats)
    turned = []
    for t in range(3):
        turned += chain.run(functools.partial(turn, t=t), place, *pieces_two)
        if stats.others:
            stats.hop()
    stats_two = stats.finish()
    slope, normed_two, dpool, sums_two, head_send, head_keep = chain.run(
        functools.partial(head_step, area=area, classes=CLASSES),
        near, second_map, cat_one, stats_two, stats_one, norm_gain, norm_bias, info, head_lowered, bias_row,
    )
    sums_two = Sum(chain, sums_two)
    recv = swap(head_send.value, "rep", 1)
    sums_two.hop()
    head_send, head_keep = chain.run(head_split, far_side, head_keep, recv)
    recv = swap(head_send.value, "rep", 2)
    sums_two.hop()
    (head_keep,) = chain.run(merge, head_keep, recv)
    head_groups = [("dp", [1]), ("dp", [2, 4])] if ndp == 8 else [("dp", [b]) for b in bits_of(ndp)]
    head_sum = Sum(chain, head_keep, head_groups)
    head_sum.hop()
    sums_two.finish()
    (hidden_two,) = chain.run(
        functools.partial(back_two, area=area, nrep=nrep),
        near, slope, dpool, normed_two, stats_two, stats_one, norm_gain, sums_two.x, info,
    )
    head_pack = head_sum.finish()
    head_other = swap(head_pack.value, "rep", 2)
    grads = functools.partial(start_grads, chain, side=map_side, nrep=nrep, ndp=ndp)
    two = [None] * 3
    (two[2],) = grads("two", cat_two, hidden_two, kys=(2,))
    (head_pack,) = chain.run(head_join, far_side, head_pack, head_other)
    head_other = swap(head_pack.value, "rep", 1)
    two[0], two[1] = grads("two", cat_two, hidden_two, kys=(0, 1))
    (head_pack,) = chain.run(head_join, near, head_pack, head_other)
    two[2].step()
    two[0].step()
    two[1].step()
    up_one, up_two, sums_one = chain.run(
        functools.partial(act_grad, side=map_side, nrep=nrep),
        near, hidden_two, *turned, normed_one, norm_gain, norm_bias,
    )
    sums_one = Sum(chain, sums_one)
    sums_one.hop()
    two[1].step()
    sums_one.hop()
    two[0].step()
    sums_one.finish()
    two[2].step()
    (hidden_one,) = chain.run(
        functools.partial(back_one, area=area, nrep=nrep),
        near, up_one, up_two, normed_one, stats_one, norm_gain, sums_one.x, info,
    )
    border = (TASKS - 1) * CLASSES
    (small_pair,) = chain.run(functools.partial(small_dots, border=border), sums_one.x, sums_two.x, head_pack)
    one = [None] * 3
    (one[2],) = grads("one", cat_one, hidden_one, kys=(2,))
    two[1].step()
    two[0].step()
    one[0], one[1] = grads("one", cat_one, hidden_one, kys=(0, 1))
    one[2].step()
    one[0].step()
    one[1].step()
    two[2].step_late()
    two[1].step_late()
    two[0].step_late()
    one[2].step_late()
    one[1].step_late()
    one[0].step_late()
    two[2].step_late()
    one[2].step_late()
    one[1].step_late()
    one[0].step_late()
    one[2].step_late()
    one[1].step_late()
    one[0].step_late()
    while any(x.order for x in one + two):
        for x in two + one:
            if x.order:
                x.step_late()
    *shares, partial_value = chain.run(dots, *[x.keep for x in one + two], *[x.recv for x in one + two])
    shares = [b.value for b in shares]
    partial_value = partial_value.value
    partial_value = exchange_far(partial_value, ndp)
    agreement = jnp.sum(exchange_near(partial_value, ndp) + small_pair.value, axis=1)
    project_coef = jnp.minimum(agreement[0], 0.0) / agreement[1]
    dp_keys = [("dp", b) for b in reversed(bits_of(ndp))]
    ways = (dp_keys, dp_keys[:1] + dp_keys[-1:] + dp_keys[1:-1])
    parts = []
    for l, way in enumerate(ways):
        x = project(project_coef.reshape(1), *shares[3 * l : 3 * l + 3])
        with jax.named_scope(f"whole{l}"):
            parts.append(gather_dp(x, [], way[:-1], ndp))
    late = (project_coef.reshape(1), conv_master)
    (coef_late, master_late), parts = after(late, parts)
    weight_part = weight_squares(master_late)
    small = small_update(
        coef_late, head_pack.value, sums_one.x.value, sums_two.x.value, head_master, head_rows[None], head_cols[None],
        head_bias[None], head_bias_moment[None], norm_gain, norm_bias, norm_moment.reshape(4, channels), decay=decay_rate,
    )
    for l, way in enumerate(ways):
        names = sorted(way[:-1], key=dp_keys.index)
        with jax.named_scope(f"whole{l}"):
            part = gather_dp(parts[l], names, way[-1:], ndp)
        parts[l] = part.reshape((ndp,) + part.shape[-3:])
    conv_cols_new, row_part = measure_rows(conv_cols, *parts, decay=decay_rate)
    count_rows = conv_master.shape[1]
    row_pack = jnp.concatenate([row_part.reshape(2, -1), weight_part], axis=1)
    row_pack = axis_sum(row_pack, "rep")
    row_total = row_pack[:, :count_rows]
    over_total = row_pack[:, count_rows : 2 * count_rows]
    weight_total = row_pack[:, 2 * count_rows]
    conv_rows_new = decay_rate * conv_rows + (1.0 - decay_rate) * (row_total / channels + eps_one)
    row_mean = jnp.mean(conv_rows_new, axis=1)
    entries = count_rows * channels
    update_rms = jnp.sqrt(row_mean * jnp.sum(over_total / conv_rows_new, axis=1) / entries)
    step_size = rel_step * jnp.maximum(eps_two, jnp.sqrt(weight_total / entries))
    step_size = step_size / jnp.maximum(1.0, update_rms / clip_level)
    row_factor = lax.rsqrt(conv_rows_new / row_mean[:, None])
    col_factor = lax.rsqrt(conv_cols_new) * step_size[:, None]
    conv_grad, conv_new, conv_copy_new = update(conv_master, row_factor[:, None], col_factor[:, None], *parts)
    (
        head_grad,
        head_rows_new,
        head_cols_new,
        head_new,
        head_copy_new,
        bias_grad,
        bias_moment_new,
        bias_new,
        norm_grad,
        norm_moment_new,
        norm_new,
        losses,
    ) = small
    totals = stats_one.value[2, :3]
    cur_losses = jnp.stack([losses[0, 0], totals[1]])
    mem_losses = jnp.stack([losses[1, 0], totals[2]])
    return (
        cur_losses,
        mem_losses,
        agreement,
        conv_grad,
        conv_rows_new,
        conv_cols_new,
        conv_new,
        conv_copy_new,
        head_grad,
        head_rows_new[0],
        head_cols_new[0],
        head_new,
        head_copy_new,
        bias_grad[0],
        bias_moment_new[0],
        bias_new[0],
        norm_grad.reshape(norm_moment.shape),
        norm_moment_new.reshape(norm_moment.shape),
        norm_new.reshape(norm_moment.shape),
    )


def solution(mesh):
    nrep = mesh.shape["rep"]
    ndp = mesh.shape["dp"]

    def run(*args):
        return local(nrep, ndp, *args)

    return jax.shard_map(
        run,
        mesh=mesh,
        in_specs=(
            P(("dp", "rep"), None, None, None),
            P(("dp", "rep")),
            P(("dp", "rep")),
            P(("dp", "rep")),
            P(("dp", "rep")),
            P(),
            P(None, None, "rep"),
            P(),
            P(None, "rep"),
            P(),
            P(),
            P(),
            P(),
            P(),
            P(),
            P(),
            P(),
        ),
        out_specs=(
            P(),
            P(),
            P(),
            P(None, None, "rep"),
            P(),
            P(None, "rep"),
            P(None, None, "rep"),
            P(None, None, "rep"),
            P(),
            P(),
            P(),
            P(),
            P(),
            P(),
            P(),
            P(),
            P(),
            P(),
            P(),
        ),
        check_vma=False,
    )
```
